256 devices in a mesh: pipe: 8 (over x, core), expert: 32 (over z, y).
Axes of the slice: x: 4, y: 4, z: 8, core: 2. Of those that a mesh axis runs over, the one named last changes fastest.
Arguments:
- enter_fwd: bfloat16 [1, 1024, 2048], P(None, 'expert'), may hold values from -6 to 6
- held_fwd: bfloat16 [8, 1024, 2048], P('pipe', 'expert'), may hold values from -6 to 6
- route_fwd: int32 [2, 8, 1024, 8], P(None, 'pipe', 'expert'), may hold values from 0 to 31, all different within a row; in each aligned block of 32 rows (0 to 31, 32 to 63, ..., all dimensions but the last counted through in order) at most 9 rows name the same one
- prob_fwd: float32 [2, 8, 1024, 8], P(None, 'pipe', 'expert'), may hold values from 0.02 to 0.3
- enter_grad: bfloat16 [1, 1024, 2048], P(None, 'expert'), may hold values from -6 to 6
- held_grad: bfloat16 [8, 1024, 2048], P('pipe', 'expert'), may hold values from -6 to 6
- saved_inputs: bfloat16 [2, 8, 1024, 2048], P(None, 'pipe', 'expert'), may hold values from -6 to 6
- route_grad: int32 [2, 8, 1024, 8], P(None, 'pipe', 'expert'), may hold values from 0 to 31, all different within a row; in each aligned block of 32 rows (0 to 31, 32 to 63, ..., all dimensions but the last counted through in order) at most 9 rows name the same one
- prob_grad: float32 [2, 8, 1024, 8], P(None, 'pipe', 'expert'), may hold values from 0.02 to 0.3
- norm_gain: float32 [8, 2048], P('pipe'), may hold values from 0.1 to 1.9
- w_gate: bfloat16 [8, 32, 2048, 768], P('pipe', 'expert'), may hold values from -0.125 to 0.125
- w_up: bfloat16 [8, 32, 2048, 768], P('pipe', 'expert'), may hold values from -0.125 to 0.125
- w_down: bfloat16 [8, 32, 768, 2048], P('pipe', 'expert'), may hold values from -0.21875 to 0.21875
Outputs:
- layer_outputs: bfloat16 [2, 8, 1024, 2048], P(None, 'pipe', 'expert')
- input_grads: bfloat16 [2, 8, 1024, 2048], P(None, 'pipe', 'expert')
The draws below stay inside these ranges and needn't reach their ends.
Inputs may be any that keep to these rules, and one draw needn't show every extreme that they name: `route_fwd`: within the 32 tokens i * 32 .. (i + 1) * 32 - 1 of one step and section, no expert is named by more than 9 tokens, and a token names 8 different experts. `route_grad`: within the 32 tokens i * 32 .. (i + 1) * 32 - 1 of one step and section, no expert is named by more than 9 tokens, and a token names 8 different experts.
All inputs are finite; a program needn't handle non-finite values.
Results may differ from the reference program's by a relative error of at most 0.007.
Values may be sent and summed in bfloat16 or wider, within the bound.
No kernel may reach another device: no remote copies, remote signals or barrier semaphores. Data moves between devices by JAX's collectives and lax.ppermute only.
A program may use at most 128 MiB of HBM per device.

```python
import math
import jax
import jax.numpy as jnp
import numpy as np
from jax import lax

D = 2048
FF = 768
TOP = 8
TOK_DEV = 32
STEPS = 2
EXPERTS = 32
TOKENS = 1024
CAP = 9
N_PIPE = 8


def block_scale(key, dims, shards, low, top_value):
    def one(axis_at, parts):
        heights = jax.random.uniform(jax.random.fold_in(jax.random.fold_in(key, 6), axis_at), (parts,), jnp.float32, low / len(shards), top_value / len(shards))
        return jnp.repeat(jnp.exp(heights), dims[axis_at] // parts).reshape((-1,) + (1,) * (len(dims) - axis_at - 1))

    loudness = one(*shards[0])
    for cut in shards[1:]:
        loudness = loudness * one(*cut)
    return loudness


def shared_out(own_key, own, number, rows, amount, top, limit, lean):
    sequence = jax.random.permutation(own_key, amount)
    packed, common = portions_of(amount, rows * top, limit, lean, True), portions_of(amount, rows * top, limit, lean, False)
    places = jnp.arange(amount)

    def named(tallies, offset_by):
        used = int((tallies > 0).sum())
        fixed = max(1, used // 4)
        passed = fixed + (places - fixed + offset_by * (used - fixed)) % max(1, amount - fixed)
        return jnp.zeros((amount,), jnp.int32).at[sequence[jnp.where(places < fixed, places, passed)]].set(jnp.asarray(tallies, jnp.int32))

    tallies = jnp.where(number % 4 == 0, named(packed, number // 4), named(common, number - number // 4 - 1))
    mixed = jax.random.permutation(jax.random.fold_in(own, 3), amount)
    donor, taker = mixed[0:amount // 2 * 2:2], mixed[1:amount // 2 * 2:2]
    margin = jnp.minimum(tallies[donor] - 1, limit - tallies[taker]) // 2
    margin = jnp.where((donor == sequence[0]) | (taker == sequence[0]) | (tallies[taker] == 0), 0, jnp.maximum(margin, 0))
    passed = jax.random.randint(jax.random.fold_in(own, 4), (amount // 2,), 0, 1 << 20) % (margin + 1)
    tallies = tallies.at[donor].add(-passed).at[taker].add(passed)
    labels = jnp.searchsorted(jnp.cumsum(tallies), jnp.arange(rows * top), side="right").astype(jnp.int32)
    grid = labels.reshape(top, rows).T
    grid = grid[jax.random.permutation(jax.random.fold_in(own, 1), rows)]
    offset_by = jax.random.randint(jax.random.fold_in(own, 2), (rows, 1), 0, top)
    return jnp.take_along_axis(grid, (jnp.arange(top)[None, :] + offset_by) % top, axis=1)


def portions_of(amount, total, bound, skew, full):
    weights = [(1 << 20) // math.isqrt(rank ** skew) + 1 for rank in range(1, amount + 1)]
    largest = bound if full else min(bound, max(-(-total // amount), total * weights[0] // sum(weights)))
    least = 1 if total - largest >= amount - 1 else 0
    holding, rest = [largest] + [least] * (amount - 1), total - largest - least * (amount - 1)
    while rest > 0:
        candidates = [i for i in range(1, amount) if holding[i] < largest] or [i for i in range(1, amount) if holding[i] < bound]
        pool, left = sum([weights[i] for i in candidates]), rest
        for i in candidates:
            extra = min(bound - holding[i], max(1, left * weights[i] // pool), rest)
            holding[i] = holding[i] + extra
            rest = rest - extra
    return np.array(holding)


def normal_values(rng, extent, scale, limit, cuts=(), held_as=jnp.bfloat16):
    level = block_scale(rng, extent, cuts, -0.22, 0.18) if cuts else 1.0
    array = jax.random.normal(rng, extent, jnp.float32) * scale * level
    return jnp.minimum(jnp.maximum(array, -limit), limit).astype(held_as)


def setup_inputs(seed: int = 0) -> dict:
    seeds = jax.random.split(jax.random.key(seed), 14)
    enter_fwd = normal_values(seeds[0], (STEPS - 1, TOKENS, D), 1.0, 6.0, ((1, 32),))
    held_fwd = normal_values(seeds[1], (N_PIPE, TOKENS, D), 1.0, 6.0, ((0, 8), (1, 32)))
    route_fwd_keys = jax.random.split(jax.random.fold_in(seeds[2], 1), STEPS * N_PIPE * TOKENS // TOK_DEV)
    route_fwd_turns = jax.random.permutation(jax.random.fold_in(seeds[2], 3), STEPS * N_PIPE * TOKENS // TOK_DEV)
    route_fwd = jax.vmap(lambda own, number: shared_out(jax.random.fold_in(seeds[2], 2), own, number, TOK_DEV, EXPERTS, TOP, CAP, 2))(route_fwd_keys, route_fwd_turns).reshape((STEPS, N_PIPE, TOKENS, TOP))
    prob_fwd = jnp.clip(jnp.exp(math.log(0.3) - 2.7080503 * jax.random.uniform(seeds[3], (STEPS, N_PIPE, TOKENS, TOP), jnp.float32) ** block_scale(seeds[3], (STEPS, N_PIPE, TOKENS, TOP), ((1, 8), (2, 32)), -0.2, 0.2)), 0.02, 0.3)
    enter_grad = normal_values(seeds[4], (STEPS - 1, TOKENS, D), 1.0, 6.0, ((1, 32),))
    held_grad = normal_values(seeds[5], (N_PIPE, TOKENS, D), 1.0, 6.0, ((0, 8), (1, 32)))
    saved_inputs = normal_values(seeds[6], (STEPS, N_PIPE, TOKENS, D), 1.0, 6.0, ((1, 8), (2, 32)))
    route_grad_keys = jax.random.split(jax.random.fold_in(seeds[7], 1), STEPS * N_PIPE * TOKENS // TOK_DEV)
    route_grad_turns = jax.random.permutation(jax.random.fold_in(seeds[7], 3), STEPS * N_PIPE * TOKENS // TOK_DEV)
    route_grad = jax.vmap(lambda own, number: shared_out(jax.random.fold_in(seeds[7], 2), own, number, TOK_DEV, EXPERTS, TOP, CAP, 2))(route_grad_keys, route_grad_turns).reshape((STEPS, N_PIPE, TOKENS, TOP))
    prob_grad = jnp.clip(jnp.exp(math.log(0.3) - 2.7080503 * jax.random.uniform(seeds[8], (STEPS, N_PIPE, TOKENS, TOP), jnp.float32) ** block_scale(seeds[8], (STEPS, N_PIPE, TOKENS, TOP), ((1, 8), (2, 32)), -0.2, 0.2)), 0.02, 0.3)
    norm_gain = jnp.clip(1.0 + 0.18 * jax.random.normal(seeds[9], (N_PIPE, D), jnp.float32), 0.1, 1.9)
    w_gate = normal_values(seeds[10], (N_PIPE, EXPERTS, D, FF), D ** -0.5, 0.125, ((0, 8), (1, 32)))
    w_up = normal_values(seeds[11], (N_PIPE, EXPERTS, D, FF), D ** -0.5, 0.125, ((0, 8), (1, 32)))
    w_down = normal_values(seeds[12], (N_PIPE, EXPERTS, FF, D), FF ** -0.5, 0.21875, ((0, 8), (1, 32)))
    return {"enter_fwd": enter_fwd, "held_fwd": held_fwd, "route_fwd": route_fwd, "prob_fwd": prob_fwd, "enter_grad": enter_grad, "held_grad": held_grad, "saved_inputs": saved_inputs, "route_grad": route_grad, "prob_grad": prob_grad, "norm_gain": norm_gain, "w_gate": w_gate, "w_up": w_up, "w_down": w_down}


epsilon = 1e-06

def slot_numbers(route):
    blocks = route.reshape(-1, TOK_DEV * TOP)
    onehot = (blocks[:, :, None] == jnp.arange(EXPERTS, dtype=jnp.int32)[None, None, :]).astype(jnp.int32)
    ranks = jnp.cumsum(onehot, axis=1) - onehot
    return lax.optimization_barrier(jnp.sum(ranks * onehot, axis=2)).reshape(route.shape).astype(jnp.int32)

def positions(route):
    block_ids = (jnp.arange(route.shape[0], dtype=jnp.int32) // TOK_DEV).astype(jnp.int32)
    return (block_ids[:, None] * CAP + slot_numbers(route)).astype(jnp.int32)

def to_experts(values, route, where):
    buffers = jnp.zeros((EXPERTS, route.shape[0] // TOK_DEV * CAP, values.shape[-1]), values.dtype)
    return buffers.at[route, where].set(values)

def norm_scale(block):
    wide = block.astype(jnp.float32)
    scale = lax.rsqrt(lax.optimization_barrier(jnp.mean(wide * wide, axis=-1, keepdims=True)) + epsilon)
    return (wide, scale)

def expert_forward(rows, gate_w, up_w, down_w):
    gate_pre = jnp.dot(rows, gate_w, preferred_element_type=jnp.float32)
    up_pre = jnp.dot(rows, up_w, preferred_element_type=jnp.float32)
    hidden = (jax.nn.silu(gate_pre) * up_pre).astype(jnp.bfloat16)
    return jnp.dot(hidden, down_w, preferred_element_type=jnp.float32).astype(jnp.bfloat16)

def expert_backward(rows, grad_rows, gate_w, up_w, down_w):
    gate_pre = jnp.dot(rows, gate_w, preferred_element_type=jnp.float32)
    up_pre = jnp.dot(rows, up_w, preferred_element_type=jnp.float32)
    d_hidden = jnp.dot(grad_rows, down_w.T, preferred_element_type=jnp.float32)
    sigmoid = jax.nn.sigmoid(gate_pre)
    d_gate = (d_hidden * up_pre * sigmoid * (1.0 + gate_pre * (1.0 - sigmoid))).astype(jnp.bfloat16)
    d_up = (d_hidden * gate_pre * sigmoid).astype(jnp.bfloat16)
    total = jnp.dot(d_gate, gate_w.T, preferred_element_type=jnp.float32) + jnp.dot(d_up, up_w.T, preferred_element_type=jnp.float32)
    return total.astype(jnp.bfloat16)

def layer_forward(block, gain, route, prob, gate_w, up_w, down_w):
    wide, scale = norm_scale(block)
    normed = (wide * scale * gain[None, :]).astype(jnp.bfloat16)
    where = positions(route)
    spread = jnp.broadcast_to(normed[:, None, :], route.shape + (normed.shape[-1],))
    buffers = to_experts(spread, route, where)
    results = lax.map(lambda item: expert_forward(item[0], item[1], item[2], item[3]), (buffers, gate_w, up_w, down_w))
    back = results[route, where].astype(jnp.float32)
    mixed = wide + lax.optimization_barrier(jnp.sum(prob[:, :, None] * back, axis=1))
    return mixed.astype(jnp.bfloat16)

def layer_backward(block, grad, gain, route, prob, gate_w, up_w, down_w):
    wide, scale = norm_scale(block)
    normed = (wide * scale * gain[None, :]).astype(jnp.bfloat16)
    where = positions(route)
    spread = jnp.broadcast_to(normed[:, None, :], route.shape + (normed.shape[-1],))
    rows = to_experts(spread, route, where)
    weighted = (prob[:, :, None] * grad.astype(jnp.float32)[:, None, :]).astype(jnp.bfloat16)
    grad_buffers = to_experts(weighted, route, where)
    results = lax.map(lambda item: expert_backward(item[0], item[1], item[2], item[3], item[4]), (rows, grad_buffers, gate_w, up_w, down_w))
    d_normed = lax.optimization_barrier(jnp.sum(results[route, where].astype(jnp.float32), axis=1))
    scaled_u = d_normed * gain[None, :]
    inner = lax.optimization_barrier(jnp.mean(scaled_u * wide, axis=-1, keepdims=True))
    d_block = scale * scaled_u - wide * (scale * scale * scale) * inner
    return (grad.astype(jnp.float32) + d_block).astype(jnp.bfloat16)

def reference(enter_fwd, held_fwd, route_fwd, prob_fwd, enter_grad, held_grad, saved_inputs, route_grad, prob_grad, norm_gain, w_gate, w_up, w_down):
    current_fwd = [held_fwd[section] for section in range(N_PIPE)]
    current_grad = [held_grad[section] for section in range(N_PIPE)]
    outputs_all = []
    grads_all = []
    for step in range(STEPS):
        outs_fwd = [layer_forward(current_fwd[section], norm_gain[section], route_fwd[step, section], prob_fwd[step, section], w_gate[section], w_up[section], w_down[section]) for section in range(N_PIPE)]
        outs_grad = [layer_backward(saved_inputs[step, section], current_grad[section], norm_gain[section], route_grad[step, section], prob_grad[step, section], w_gate[section], w_up[section], w_down[section]) for section in range(N_PIPE)]
        outputs_all.append(jnp.stack(outs_fwd))
        grads_all.append(jnp.stack(outs_grad))
        if step + 1 < STEPS:
            current_fwd = [enter_fwd[step]] + outs_fwd[:-1]
            current_grad = outs_grad[1:] + [enter_grad[step]]
    return (jnp.stack(outputs_all), jnp.stack(grads_all))
```

```python
import jax
import jax.numpy as jnp
from jax import lax
from jax.sharding import PartitionSpec as P

STEPS = 2
CAP = 9
PARTS = 8


epsilon = 1e-06


def passed_along(block, axis, distance):
    devices = range(lax.axis_size(axis))
    route = [(i - distance, i) for i in devices if i - distance in devices]
    return lax.ppermute(block, axis, route)


def norm_rows(block, gain):
    wide = block.astype(jnp.float32)
    scale = lax.rsqrt(jnp.mean(wide * wide, axis=-1, keepdims=True) + epsilon)
    normed = (wide * scale * gain[None, :]).astype(jnp.bfloat16)
    return (wide, scale, normed)


def split_two(values):
    high = values.astype(jnp.bfloat16)
    low = (values - high.astype(jnp.float32)).astype(jnp.bfloat16)
    return high, low


def slot_tables(route, prob, experts):
    tokens, chosen = route.shape
    lanes = PARTS * tokens
    route_lanes = jnp.tile(route.T, (1, PARTS))
    prob_lanes = jnp.tile(prob.T, (1, PARTS))
    names = lax.broadcasted_iota(jnp.int32, (experts, lanes), 0)
    hit = jnp.zeros((experts, lanes), jnp.bool_)
    weight = jnp.zeros((experts, lanes), jnp.float32)
    for k in range(chosen):
        same = names == route_lanes[k][None, :]
        hit = hit | same
        weight = jnp.where(same, prob_lanes[k][None, :], weight)
    before = lax.broadcasted_iota(jnp.int32, (lanes, lanes), 0)
    after = lax.broadcasted_iota(jnp.int32, (lanes, lanes), 1)
    earlier = ((before // tokens == after // tokens) & (before < after)).astype(jnp.bfloat16)
    rank = jnp.dot(hit.astype(jnp.bfloat16), earlier, preferred_element_type=jnp.float32)
    part = lax.broadcasted_iota(jnp.int32, (experts, lanes), 1) // tokens
    key = jnp.where(hit, rank.astype(jnp.int32) * PARTS + part, -1)
    rows = lax.broadcasted_iota(jnp.int32, (experts, CAP * PARTS, lanes), 1)
    select = key[:, None, :] == rows
    return select.reshape(-1, lanes), jnp.where(select, weight[:, None, :], 0.0).reshape(-1, lanes)


def to_parts(block):
    tokens, width = block.shape
    return block.reshape(tokens, PARTS, width // PARTS).transpose(1, 0, 2).reshape(PARTS * tokens, -1)


def from_parts(block, tokens):
    return block.reshape(PARTS, tokens, -1).transpose(1, 0, 2).reshape(tokens, -1)


def picked(table, block):
    return jnp.dot(table, block, preferred_element_type=jnp.float32)


def returned(table, rows):
    return lax.dot_general(table, rows, (((0,), (0,)), ((), ())), preferred_element_type=jnp.float32)


def expert_forward(rows, gate_w, up_w, down_w):
    gate_pre = jnp.dot(rows, gate_w, preferred_element_type=jnp.float32)
    up_pre = jnp.dot(rows, up_w, preferred_element_type=jnp.float32)
    hidden = (jax.nn.silu(gate_pre) * up_pre).astype(jnp.bfloat16)
    return jnp.dot(hidden, down_w, preferred_element_type=jnp.float32).astype(jnp.bfloat16)


def expert_backward(rows, grad_rows, gate_w, up_w, down_w):
    gate_pre = jnp.dot(rows, gate_w, preferred_element_type=jnp.float32)
    up_pre = jnp.dot(rows, up_w, preferred_element_type=jnp.float32)
    d_hidden = jnp.dot(grad_rows, down_w.T, preferred_element_type=jnp.float32)
    sigmoid = jax.nn.sigmoid(gate_pre)
    d_gate = (d_hidden * up_pre * sigmoid * (1.0 + gate_pre * (1.0 - sigmoid))).astype(jnp.bfloat16)
    d_up = (d_hidden * gate_pre * sigmoid).astype(jnp.bfloat16)
    total = jnp.dot(d_gate, gate_w.T, preferred_element_type=jnp.float32) + jnp.dot(
        d_up, up_w.T, preferred_element_type=jnp.float32
    )
    return total.astype(jnp.bfloat16)


def exchanged(chunks):
    return lax.all_to_all(chunks, "expert", split_axis=0, concat_axis=0, tiled=True)


def on_device(
    enter_fwd,
    held_fwd,
    route_fwd,
    prob_fwd,
    enter_grad,
    held_grad,
    saved_inputs,
    route_grad,
    prob_grad,
    norm_gain,
    w_gate,
    w_up,
    w_down,
):
    tokens = held_fwd.shape[1]
    width = held_fwd.shape[2]
    experts = lax.axis_size("expert")
    chunk = CAP * PARTS
    gain = norm_gain[0]
    gate_w = w_gate[0, 0]
    up_w = w_up[0, 0]
    down_w = w_down[0, 0]
    section = lax.axis_index("pipe")
    last_section = lax.axis_size("pipe") - 1
    current_fwd = held_fwd[0]
    current_grad = held_grad[0]
    outputs_all = []
    grads_all = []

    def to_rows(chunks):
        return chunks.reshape(experts * CAP, width)

    def to_chunks(rows):
        return rows.reshape(experts, chunk, width // PARTS)

    for step in range(STEPS):
        select_fwd, mixing_fwd = slot_tables(route_fwd[step, 0], prob_fwd[step, 0], experts)
        wide_fwd, _, normed_fwd = norm_rows(current_fwd, gain)
        send_fwd = picked(select_fwd.astype(jnp.bfloat16), to_parts(normed_fwd)).astype(jnp.bfloat16)
        run_received = exchanged(send_fwd.reshape(experts, chunk, -1))

        select_grad, mixing_grad = slot_tables(route_grad[step, 0], prob_grad[step, 0], experts)
        select_grad = select_grad.astype(jnp.bfloat16)
        wide_saved, scale_saved, normed_saved = norm_rows(saved_inputs[step, 0], gain)
        send_saved = picked(select_grad, to_parts(normed_saved)).astype(jnp.bfloat16)
        high, low = split_two(mixing_grad)
        grad_parts = to_parts(current_grad)
        send_weighted = (picked(high, grad_parts) + picked(low, grad_parts)).astype(jnp.bfloat16)
        received = exchanged(
            jnp.concatenate(
                [send_saved.reshape(experts, chunk, -1), send_weighted.reshape(experts, chunk, -1)], axis=1
            )
        )
        run_result = expert_forward(to_rows(run_received), gate_w, up_w, down_w)
        back_fwd = exchanged(to_chunks(run_result)).reshape(experts * chunk, -1)
        result = expert_backward(
            to_rows(received[:, :chunk]), to_rows(received[:, chunk:]), gate_w, up_w, down_w
        )
        back_grad = exchanged(to_chunks(result)).reshape(experts * chunk, -1)

        high, low = split_two(mixing_fwd)
        mixed = wide_fwd + from_parts(returned(high, back_fwd) + returned(low, back_fwd), tokens)
        out_fwd = mixed.astype(jnp.bfloat16)
        d_normed = from_parts(returned(select_grad, back_grad), tokens)
        scaled_u = d_normed * gain[None, :]
        inner = jnp.mean(scaled_u * wide_saved, axis=-1, keepdims=True)
        d_block = (
            scale_saved * scaled_u - wide_saved * (scale_saved * scale_saved * scale_saved) * inner
        )
        out_grad = (current_grad.astype(jnp.float32) + d_block).astype(jnp.bfloat16)
        outputs_all.append(out_fwd[None])
        grads_all.append(out_grad[None])
        if step + 1 < STEPS:
            moved_fwd = passed_along(out_fwd, "pipe", 1)
            moved_grad = passed_along(out_grad, "pipe", -1)
            current_fwd = jnp.where(section == 0, enter_fwd[step], moved_fwd)
            current_grad = jnp.where(section == last_section, enter_grad[step], moved_grad)
    return (jnp.stack(outputs_all), jnp.stack(grads_all))


def solution(mesh):
    return jax.shard_map(
        on_device,
        mesh=mesh,
        in_specs=(
            P(None, "expert", None),
            P("pipe", "expert", None),
            P(None, "pipe", "expert", None),
            P(None, "pipe", "expert", None),
            P(None, "expert", None),
            P("pipe", "expert", None),
            P(None, "pipe", "expert", None),
            P(None, "pipe", "expert", None),
            P(None, "pipe", "expert", None),
            P("pipe", None),
            P("pipe", "expert", None, None),
            P("pipe", "expert", None, None),
            P("pipe", "expert", None, None),
        ),
        out_specs=(P(None, "pipe", "expert", None), P(None, "pipe", "expert", None)),
        check_vma=False,
    )
```

```python
import jax
import jax.numpy as jnp
from jax import lax
from jax.experimental import pallas as pl
from jax.experimental.pallas import tpu as pltpu
from jax.sharding import Mesh, PartitionSpec as P

STEPS = 2
CAP = 9
PARTS = 8
COLUMN = 4
GROUP = 80
HIDDEN_BLOCK = 256
VMEM_LIMIT = 58 * 1024 * 1024


epsilon = 1e-06


def passed_along(block, axis, distance):
    devices = range(lax.axis_size(axis))
    route = [(i - distance, i) for i in devices if i - distance in devices]
    return lax.ppermute(block, axis, route)


def turned(block, axis, distance):
    size = lax.axis_size(axis)
    return lax.ppermute(block, axis, [(i, (i + distance) % size) for i in range(size)])


def after(value, *earlier):
    return lax.optimization_barrier((value,) + earlier)[0]


def norm_rows(block, gain):
    wide = block.astype(jnp.float32)
    scale = lax.rsqrt(jnp.mean(wide * wide, axis=-1, keepdims=True) + epsilon)
    normed = (wide * scale * gain[None, :]).astype(jnp.bfloat16)
    return (wide, scale, normed)


def split_two(values):
    high = lax.reduce_precision(values, exponent_bits=8, mantissa_bits=7)
    return high.astype(jnp.bfloat16), (values - high).astype(jnp.bfloat16)


def iota(shape, axis):
    return lax.broadcasted_iota(jnp.int32, shape, axis)


def earlier_tokens(lanes, tokens):
    before, now = iota((lanes, lanes), 0), iota((lanes, lanes), 1)
    return ((before // tokens == now // tokens) & (before < now)).astype(jnp.bfloat16)


def ranked(hit, earlier):
    return jnp.dot(hit.astype(jnp.bfloat16), earlier, preferred_element_type=jnp.float32).astype(jnp.int32)


def slot_keys(route_lanes, prob_lanes, experts, tokens, earlier):
    lanes = route_lanes.shape[1]
    names = iota((experts, lanes), 0)
    hit = jnp.zeros((experts, lanes), jnp.bool_)
    weight = jnp.zeros((experts, lanes), jnp.float32)
    for k in range(route_lanes.shape[0]):
        same = names == route_lanes[k][None, :]
        hit = hit | same
        weight = jnp.where(same, prob_lanes[k][None, :], weight)
    part = iota((experts, lanes), 1) // tokens
    return jnp.where(hit, ranked(hit, earlier) * PARTS + part, -1), weight


def select_table(key, rows):
    hits = key[:, None, :] == iota((key.shape[0], rows, key.shape[1]), 1)
    return hits.astype(jnp.bfloat16).reshape(-1, key.shape[1])


def weight_table(key, weight, rows):
    hits = key[:, None, :] == iota((key.shape[0], rows, key.shape[1]), 1)
    return split_two(jnp.where(hits, weight[:, None, :], 0.0).reshape(-1, key.shape[1]))


def to_parts(block):
    tokens, width = block.shape
    return block.reshape(tokens, PARTS, width // PARTS).transpose(1, 0, 2).reshape(PARTS * tokens, -1)


def from_parts(block, tokens):
    return block.reshape(PARTS, tokens, -1).transpose(1, 0, 2).reshape(tokens, -1)


def picked(table, block):
    return jnp.dot(table, block, preferred_element_type=jnp.float32)


def dot_nn(a, b):
    return jnp.dot(a, b, preferred_element_type=jnp.float32)


def dot_nt(a, b):
    return lax.dot_general(a, b, (((1,), (1,)), ((), ())), preferred_element_type=jnp.float32)


def regroup(parts, rows, group):
    size = parts * group
    to, come = iota((size, size), 0), iota((size, size), 1)
    part, row = to // group, to % group
    source, place = come // group, come % group
    same = (source == row // CAP) & (place == (row % CAP) * parts + part) & (row < rows)
    return same.astype(jnp.bfloat16)


def rows_from_chunks(chunks_ref, column, table_ref, stage_ref, rows_ref, at):
    layers_z, _, real, part = chunks_ref.shape
    for z in range(layers_z):
        stage_ref[z * GROUP : z * GROUP + real, :] = chunks_ref[z, column]
    placed = dot_nn(table_ref[...], stage_ref[...]).astype(jnp.bfloat16)
    for c in range(PARTS):
        rows_ref[at : at + GROUP, c * part : (c + 1) * part] = placed[c * GROUP : (c + 1) * GROUP]


def rows_to_chunks(total_ref, at, table_ref, stage_ref, out_ref, column):
    layers_z, _, real, part = out_ref.shape
    for c in range(PARTS):
        stage_ref[c * GROUP : (c + 1) * GROUP, :] = total_ref[
            at : at + GROUP, c * part : (c + 1) * part
        ].astype(jnp.bfloat16)
    placed = lax.dot_general(
        table_ref[...], stage_ref[...], (((0,), (0,)), ((), ())), preferred_element_type=jnp.float32
    ).astype(jnp.bfloat16)
    for z in range(layers_z):
        out_ref[z, column] = placed[z * GROUP : z * GROUP + real]


def add_share(total_ref, share):
    @pl.when(pl.program_id(0) == 0)
    def _():
        total_ref[...] = share

    @pl.when(pl.program_id(0) > 0)
    def _():
        total_ref[...] += share


def forward_kernel(chunks_ref, table_ref, gate_ref, up_ref, down_ref, out_ref, rows_ref, total_ref, stage_ref):
    layers_y = chunks_ref.shape[1]

    @pl.when(pl.program_id(0) == 0)
    def _():
        stage_ref[...] = jnp.zeros_like(stage_ref)
        for y in range(layers_y):
            rows_from_chunks(chunks_ref, y, table_ref, stage_ref, rows_ref, y * GROUP)

    rows = rows_ref[...]
    gate = dot_nn(rows, gate_ref[...])
    up = dot_nn(rows, up_ref[...])
    hidden = (gate * jax.nn.sigmoid(gate) * up).astype(jnp.bfloat16)
    add_share(total_ref, dot_nn(hidden, down_ref[...]))

    @pl.when(pl.program_id(0) == pl.num_programs(0) - 1)
    def _():
        for y in range(layers_y):
            rows_to_chunks(total_ref, y * GROUP, table_ref, stage_ref, out_ref, y)


def backward_kernel(
    y_ref, x0, x1, x2, x3, chunks_ref, table_ref, gate_ref, up_ref, down_ref, out_ref, rows_ref, grads_ref, total_ref, stage_ref
):
    real = x0.shape[0]
    layers_y = chunks_ref.shape[1]

    @pl.when(pl.program_id(0) == 0)
    def _():
        rows_ref[...] = jnp.zeros_like(rows_ref)
        stage_ref[...] = jnp.zeros_like(stage_ref)
        for d, x in enumerate((x0, x1, x2, x3)):
            rows_ref[d * GROUP : d * GROUP + real, :] = x[...]
            column = (y_ref[0] + layers_y - d) % layers_y
            rows_from_chunks(chunks_ref, column, table_ref, stage_ref, grads_ref, d * GROUP)

    rows = rows_ref[...]
    gate = dot_nn(rows, gate_ref[...])
    up = dot_nn(rows, up_ref[...])
    d_hidden = dot_nt(grads_ref[...], down_ref[...])
    sigmoid = jax.nn.sigmoid(gate)
    d_gate = (d_hidden * up * sigmoid * (1.0 + gate * (1.0 - sigmoid))).astype(jnp.bfloat16)
    d_up = (d_hidden * gate * sigmoid).astype(jnp.bfloat16)
    add_share(total_ref, dot_nt(d_gate, gate_ref[...]) + dot_nt(d_up, up_ref[...]))

    @pl.when(pl.program_id(0) == pl.num_programs(0) - 1)
    def _():
        for d in range(layers_y):
            column = (y_ref[0] + layers_y - d) % layers_y
            rows_to_chunks(total_ref, d * GROUP, table_ref, stage_ref, out_ref, column)


def weight_specs(width, hidden):
    return [
        pl.BlockSpec((width, HIDDEN_BLOCK), lambda j, *_: (0, j)),
        pl.BlockSpec((width, HIDDEN_BLOCK), lambda j, *_: (0, j)),
        pl.BlockSpec((HIDDEN_BLOCK, width), lambda j, *_: (j, 0)),
    ]


def whole(shape):
    return pl.BlockSpec(shape, lambda j, *_: (0,) * len(shape))


def expert_forward(chunks, table, gate_w, up_w, down_w):
    width, hidden = gate_w.shape
    total = chunks.shape[1] * GROUP
    return pl.pallas_call(
        forward_kernel,
        grid=(hidden // HIDDEN_BLOCK,),
        in_specs=[whole(chunks.shape), whole(table.shape)] + weight_specs(width, hidden),
        out_specs=whole(chunks.shape),
        out_shape=jax.ShapeDtypeStruct(chunks.shape, jnp.bfloat16),
        scratch_shapes=[
            pltpu.VMEM((total, width), jnp.bfloat16),
            pltpu.VMEM((total, width), jnp.float32),
            pltpu.VMEM((PARTS * GROUP, chunks.shape[3]), jnp.bfloat16),
        ],
        compiler_params=pltpu.CompilerParams(vmem_limit_bytes=VMEM_LIMIT),
        cost_estimate=pl.CostEstimate(
            flops=6 * total * width * hidden, bytes_accessed=6 * width * hidden, transcendentals=total * hidden
        ),
        name="expert_forward",
    )(chunks, table, gate_w, up_w, down_w)


def expert_backward(column, blocks, chunks, table, gate_w, up_w, down_w):
    real, width = blocks[0].shape
    hidden = gate_w.shape[1]
    total = len(blocks) * GROUP
    part = chunks.shape[3]
    return pl.pallas_call(
        backward_kernel,
        grid_spec=pltpu.PrefetchScalarGridSpec(
            num_scalar_prefetch=1,
            grid=(hidden // HIDDEN_BLOCK,),
            in_specs=[whole((real, width))] * 4
            + [whole(chunks.shape), whole(table.shape)]
            + weight_specs(width, hidden),
            out_specs=whole(chunks.shape),
            scratch_shapes=[
                pltpu.VMEM((total, width), jnp.bfloat16),
                pltpu.VMEM((total, width), jnp.bfloat16),
                pltpu.VMEM((total, width), jnp.float32),
                pltpu.VMEM((PARTS * GROUP, part), jnp.bfloat16),
            ],
        ),
        out_shape=jax.ShapeDtypeStruct(chunks.shape, jnp.bfloat16),
        compiler_params=pltpu.CompilerParams(vmem_limit_bytes=VMEM_LIMIT),
        cost_estimate=pl.CostEstimate(
            flops=10 * total * width * hidden, bytes_accessed=6 * width * hidden, transcendentals=total * hidden
        ),
        name="expert_backward",
    )(column, *blocks, chunks, table, gate_w, up_w, down_w)


def pick_kernel(key_ref, *refs):
    blocks, outs, source_ref = refs[:-5], refs[-5:-1], refs[-1]
    at = 0
    for block in blocks:
        source_ref[at : at + block.shape[0], :] = block[...]
        at += block.shape[0]
    lanes = key_ref.shape[1]
    slots = iota((GROUP, lanes), 0)
    table = jnp.concatenate([(key_ref[d : d + 1, :] == slots) for d in range(len(outs))], axis=0)
    rows = dot_nn(table.astype(jnp.bfloat16), source_ref[...])
    for d, out in enumerate(outs):
        out[...] = rows[d * GROUP : d * GROUP + out.shape[0]].astype(jnp.bfloat16)


def column_pick(key, blocks, real):
    width = blocks[0].shape[1]
    lanes = key.shape[1]
    return pl.pallas_call(
        pick_kernel,
        out_shape=[jax.ShapeDtypeStruct((real, width), jnp.bfloat16)] * 4,
        scratch_shapes=[pltpu.VMEM((lanes, width), jnp.bfloat16)],
        compiler_params=pltpu.CompilerParams(vmem_limit_bytes=VMEM_LIMIT),
        cost_estimate=pl.CostEstimate(flops=8 * GROUP * lanes * width, bytes_accessed=4 * lanes * width, transcendentals=0),
        name="column_pick",
    )(key, *blocks)


def on_device(
    enter_fwd,
    held_fwd,
    route_fwd,
    prob_fwd,
    enter_grad,
    held_grad,
    saved_inputs,
    route_grad,
    prob_grad,
    norm_gain,
    w_gate,
    w_up,
    w_down,
):
    tokens = held_fwd.shape[1]
    width = held_fwd.shape[2]
    layers_z, layers_y = lax.axis_size("z"), lax.axis_size("y")
    at_z, at_y = lax.axis_index("z"), lax.axis_index("y")
    experts = layers_z * layers_y
    lanes = PARTS * tokens
    chunk = CAP * PARTS
    part = width // PARTS
    gain = norm_gain[0]
    gate_w, up_w, down_w = w_gate[0, 0], w_up[0, 0], w_down[0, 0]
    section = lax.axis_index("pipe")
    last_section = lax.axis_size("pipe") - 1

    def exchanged(chunks):
        return lax.all_to_all(chunks, ("z", "y"), split_axis=0, concat_axis=0, tiled=True)

    spread = (iota((tokens, lanes), 0) == iota((tokens, lanes), 1) % tokens).astype(jnp.bfloat16)
    choices = route_fwd.shape[-1]
    routes = jnp.concatenate([route_fwd[:, 0], route_grad[:, 0]]).transpose(0, 2, 1).reshape(-1, tokens)
    routes = routes.astype(jnp.bfloat16)
    probs = jnp.concatenate([prob_fwd[:, 0], prob_grad[:, 0]]).transpose(0, 2, 1).reshape(-1, tokens)
    earlier = earlier_tokens(lanes, tokens)
    column_owner = at_z * layers_y + (at_y + iota((layers_y, lanes), 0)) % layers_y

    wide_saved, scale_saved, normed_saved = norm_rows(
        saved_inputs[:, 0].reshape(STEPS * tokens, width), gain
    )
    place = (iota((tokens, lanes), 0) + at_z * tokens == iota((tokens, lanes), 1)).astype(jnp.bfloat16)
    notes = jnp.dot(routes[STEPS * choices :], place, preferred_element_type=jnp.float32)
    notes = notes.astype(jnp.bfloat16).reshape(STEPS, choices, lanes)
    notes = jnp.concatenate(list(notes) + [jnp.zeros((choices, width - STEPS * lanes), jnp.bfloat16)], axis=1)
    first = jnp.concatenate([normed_saved[:tokens], notes])
    first_gathered = lax.all_gather(first, "z")
    saved_routes = jnp.sum(first_gathered[:, tokens:, : STEPS * lanes].astype(jnp.float32), axis=0)
    saved_routes = saved_routes.astype(jnp.int32)
    saved_gathered = [first_gathered[:, :tokens].reshape(lanes, width)] + [
        lax.all_gather(
            after(normed_saved[step * tokens : (step + 1) * tokens], first_gathered), "z", axis=0, tiled=True
        )
        for step in range(1, STEPS)
    ]

    route_lanes = jnp.dot(after(routes, first), spread, preferred_element_type=jnp.float32)
    route_lanes = route_lanes.astype(jnp.int32).reshape(2 * STEPS, choices, lanes)
    prob_lanes = jnp.dot(probs, spread.astype(jnp.float32), precision=lax.Precision.HIGHEST)
    prob_lanes = prob_lanes.reshape(2 * STEPS, choices, lanes)

    def column_keys(route):
        hit = jnp.zeros((layers_y, lanes), jnp.bool_)
        for k in range(choices):
            hit = hit | (column_owner == route[k][None, :])
        block = iota((layers_y, lanes), 1) // tokens
        return jnp.where(hit, ranked(hit, earlier) + block * CAP, -1)

    def column_sent(rows, way):
        return [rows[0]] + [turned(rows[d], "y", way * d) for d in range(1, layers_y)]

    def saved_rows(step, *earlier):
        key = column_keys(saved_routes[:, step * lanes : (step + 1) * lanes])
        return column_sent(column_pick(after(key, *earlier), [saved_gathered[step]], layers_z * CAP), 1)

    def forward_send(block, step):
        wide, _, normed = norm_rows(block, gain)
        key, weight = slot_keys(route_lanes[step], prob_lanes[step], experts, tokens, earlier)
        send = picked(select_table(key, chunk), to_parts(normed)).astype(jnp.bfloat16)
        mixing = tuple(t.T for t in weight_table(key, weight, chunk))
        return wide, mixing, send.reshape(experts, chunk, part)

    def grad_send(block, step):
        key, weight = slot_keys(
            route_lanes[STEPS + step], prob_lanes[STEPS + step], experts, tokens, earlier
        )
        high, low = weight_table(key, weight, chunk)
        parts = to_parts(block)
        send = (picked(high, parts) + picked(low, parts)).astype(jnp.bfloat16)
        return select_table(key, chunk).T, send.reshape(experts, chunk, part)

    def forward_out(wide, mixing, back):
        high, low = mixing
        back = back.reshape(experts * chunk, part)
        return (wide + from_parts(picked(high, back) + picked(low, back), tokens)).astype(jnp.bfloat16)

    def grad_out(block, select, step, back):
        d_normed = from_parts(picked(select, back.reshape(experts * chunk, part)), tokens)
        mine = slice(step * tokens, (step + 1) * tokens)
        wide, scale = wide_saved[mine], scale_saved[mine]
        scaled_u = d_normed * gain[None, :]
        inner = jnp.mean(scaled_u * wide, axis=-1, keepdims=True)
        d_block = scale * scaled_u - wide * (scale * scale * scale) * inner
        return (block.astype(jnp.float32) + d_block).astype(jnp.bfloat16)

    table = regroup(PARTS, layers_z * CAP, GROUP)
    column = at_y.astype(jnp.int32).reshape(1)
    block_fwd, block_grad = held_fwd[0], held_grad[0]
    outputs_all, grads_all = [], []
    grid = (layers_z, layers_y, chunk, part)
    wide, mixing, send_fwd = forward_send(block_fwd, 0)
    send_fwd = after(send_fwd, first)
    select, send_grad = grad_send(block_grad, 0)
    come_saved = saved_rows(0)
    mixing, select, table, send_grad = lax.optimization_barrier((mixing, select, table, send_grad))
    for step in range(STEPS):
        more = step + 1 < STEPS
        come_fwd = exchanged(send_fwd)
        come_grad = exchanged(after(send_grad, come_fwd))
        result_fwd = expert_forward(come_fwd.reshape(grid), table, gate_w, up_w, down_w)
        back_fwd = exchanged(after(result_fwd.reshape(send_fwd.shape), come_grad, come_saved))
        result_grad = expert_backward(column, come_saved, come_grad.reshape(grid), table, gate_w, up_w, down_w)
        back_grad = exchanged(after(result_grad.reshape(send_grad.shape), back_fwd))
        out_fwd = forward_out(wide, mixing, back_fwd)
        outputs_all.append(out_fwd[None])
        if more:
            moved_fwd = passed_along(out_fwd, "pipe", 1)
            block_fwd = jnp.where(section == 0, enter_fwd[step], moved_fwd)
            wide, mixing, send_fwd = forward_send(block_fwd, step + 1)
            back_grad, send_fwd = lax.optimization_barrier((back_grad, after(send_fwd, saved_gathered[step + 1])))
            come_saved = saved_rows(step + 1, back_fwd)
        out_grad = grad_out(block_grad, select, step, back_grad)
        grads_all.append(out_grad[None])
        if more:
            moved_grad = passed_along(out_grad, "pipe", -1)
            block_grad = jnp.where(section == last_section, enter_grad[step], moved_grad)
            select, send_grad = grad_send(block_grad, step + 1)
            send_grad = after(send_grad, come_saved)
    return (jnp.stack(outputs_all), jnp.stack(grads_all))


def solution(mesh):
    sections, owners = mesh.devices.shape
    grid = Mesh(mesh.devices.reshape(sections, owners // COLUMN, COLUMN), ("pipe", "z", "y"))
    expert = ("z", "y")
    return jax.shard_map(
        on_device,
        mesh=grid,
        in_specs=(
            P(None, expert, None),
            P("pipe", expert, None),
            P(None, "pipe", expert, None),
            P(None, "pipe", expert, None),
            P(None, expert, None),
            P("pipe", expert, None),
            P(None, "pipe", expert, None),
            P(None, "pipe", expert, None),
            P(None, "pipe", expert, None),
            P("pipe", None),
            P("pipe", expert, None, None),
            P("pipe", expert, None, None),
            P("pipe", expert, None, None),
        ),
        out_specs=(P(None, "pipe", expert, None), P(None, "pipe", expert, None)),
        check_vma=False,
    )
```

```python
import functools

import jax
import jax.numpy as jnp
from jax import lax
from jax.experimental import pallas as pl
from jax.experimental.pallas import tpu as pltpu
from jax.sharding import Mesh, PartitionSpec as P

STEPS = 2
CAP = 9
PARTS = 8
COLUMN = 4
GROUP = 80
HIDDEN_BLOCK = 256
VMEM_LIMIT = 58 * 1024 * 1024


epsilon = 1e-06


def passed_along(block, axis, distance):
    devices = range(lax.axis_size(axis))
    route = [(i - distance, i) for i in devices if i - distance in devices]
    return lax.ppermute(block, axis, route)


def turned(block, axis, distance):
    size = lax.axis_size(axis)
    return lax.ppermute(block, axis, [(i, (i + distance) % size) for i in range(size)])


def after(value, *earlier):
    return lax.optimization_barrier((value,) + earlier)[0]


def norm_rows(block, gain):
    wide = block.astype(jnp.float32)
    scale = lax.rsqrt(jnp.mean(wide * wide, axis=-1, keepdims=True) + epsilon)
    normed = (wide * scale * gain[None, :]).astype(jnp.bfloat16)
    return (wide, scale, normed)


def split_two(values):
    high = lax.reduce_precision(values, exponent_bits=8, mantissa_bits=7)
    return high.astype(jnp.bfloat16), (values - high).astype(jnp.bfloat16)


def split_three(values):
    high = lax.reduce_precision(values, exponent_bits=8, mantissa_bits=7)
    middle = lax.reduce_precision(values - high, exponent_bits=8, mantissa_bits=7)
    return [t.astype(jnp.bfloat16) for t in (high, middle, values - high - middle)]


def iota(shape, axis):
    return lax.broadcasted_iota(jnp.int32, shape, axis)


def earlier_tokens(lanes, tokens):
    before, now = iota((lanes, lanes), 0), iota((lanes, lanes), 1)
    return ((before // tokens == now // tokens) & (before < now)).astype(jnp.bfloat16)


def ranked(hit, earlier):
    return jnp.dot(hit.astype(jnp.bfloat16), earlier, preferred_element_type=jnp.float32).astype(jnp.int32)


def slot_keys(route_lanes, prob_lanes, experts, tokens, earlier):
    lanes = route_lanes.shape[1]
    names = iota((experts, lanes), 0)
    hit = jnp.zeros((experts, lanes), jnp.bool_)
    weight = jnp.zeros((experts, lanes), jnp.float32)
    for k in range(route_lanes.shape[0]):
        same = names == route_lanes[k][None, :]
        hit = hit | same
        weight = jnp.where(same, prob_lanes[k][None, :], weight)
    part = iota((experts, lanes), 1) // tokens
    return jnp.where(hit, ranked(hit, earlier) * PARTS + part, -1), weight


def select_table(key, rows):
    hits = key[:, None, :] == iota((key.shape[0], rows, key.shape[1]), 1)
    return hits.astype(jnp.bfloat16).reshape(-1, key.shape[1])


def weight_table(key, weight, rows):
    hits = key[:, None, :] == iota((key.shape[0], rows, key.shape[1]), 1)
    return split_two(jnp.where(hits, weight[:, None, :], 0.0).reshape(-1, key.shape[1]))


def to_parts(block):
    tokens, width = block.shape
    return block.reshape(tokens, PARTS, width // PARTS).transpose(1, 0, 2).reshape(PARTS * tokens, -1)


def from_parts(block, tokens):
    return block.reshape(PARTS, tokens, -1).transpose(1, 0, 2).reshape(tokens, -1)


def picked(table, block):
    return jnp.dot(table, block, preferred_element_type=jnp.float32)


def dot_nn(a, b):
    return jnp.dot(a, b, preferred_element_type=jnp.float32)


def dot_nt(a, b):
    return lax.dot_general(a, b, (((1,), (1,)), ((), ())), preferred_element_type=jnp.float32)


def regroup(parts, rows, group):
    size = parts * group
    to, come = iota((size, size), 0), iota((size, size), 1)
    part, row = to // group, to % group
    source, place = come // group, come % group
    same = (source == row // CAP) & (place == (row % CAP) * parts + part) & (row < rows)
    return same.astype(jnp.bfloat16)


def rows_from_chunks(chunks_ref, column, table_ref, stage_ref, rows_ref, at):
    layers_z, _, real, part = chunks_ref.shape
    for z in range(layers_z):
        stage_ref[z * GROUP : z * GROUP + real, :] = chunks_ref[z, column]
    placed = dot_nn(table_ref[...], stage_ref[...]).astype(jnp.bfloat16)
    for c in range(PARTS):
        rows_ref[at : at + GROUP, c * part : (c + 1) * part] = placed[c * GROUP : (c + 1) * GROUP]


def rows_to_chunks(total_ref, at, table_ref, stage_ref, out_ref, column):
    layers_z, _, real, part = out_ref.shape
    for c in range(PARTS):
        stage_ref[c * GROUP : (c + 1) * GROUP, :] = total_ref[
            at : at + GROUP, c * part : (c + 1) * part
        ].astype(jnp.bfloat16)
    placed = lax.dot_general(
        table_ref[...], stage_ref[...], (((0,), (0,)), ((), ())), preferred_element_type=jnp.float32
    ).astype(jnp.bfloat16)
    for z in range(layers_z):
        out_ref[z, column] = placed[z * GROUP : z * GROUP + real]


def add_share(total_ref, share):
    @pl.when(pl.program_id(0) == 0)
    def _():
        total_ref[...] = share

    @pl.when(pl.program_id(0) > 0)
    def _():
        total_ref[...] += share


def load_rows(refs, y_ref, table_ref, stage_ref, rows_ref, real, at=0):
    for d in range(COLUMN):
        if len(refs) > 1:
            rows_ref[d * GROUP : d * GROUP + real, :] = refs[d][at : at + real, :]
        else:
            column = (y_ref[0] + COLUMN - d) % COLUMN
            rows_from_chunks(refs[0], column, table_ref, stage_ref, rows_ref, d * GROUP)


def store_rows(total_ref, y_ref, table_ref, stage_ref, out_ref):
    for d in range(COLUMN):
        column = (y_ref[0] + COLUMN - d) % COLUMN
        rows_to_chunks(total_ref, d * GROUP, table_ref, stage_ref, out_ref, column)


def forward_kernel(count, y_ref, *refs):
    rows, refs = refs[:count], refs[count:]
    table_ref, gate_ref, up_ref, down_ref, out_ref, rows_ref, total_ref, stage_ref = refs

    @pl.when(pl.program_id(0) == 0)
    def _():
        rows_ref[...] = jnp.zeros_like(rows_ref)
        stage_ref[...] = jnp.zeros_like(stage_ref)
        load_rows(rows, y_ref, table_ref, stage_ref, rows_ref, out_ref.shape[2])

    gate = dot_nn(rows_ref[...], gate_ref[...])
    up = dot_nn(rows_ref[...], up_ref[...])
    hidden = (gate * jax.nn.sigmoid(gate) * up).astype(jnp.bfloat16)
    add_share(total_ref, dot_nn(hidden, down_ref[...]))

    @pl.when(pl.program_id(0) == pl.num_programs(0) - 1)
    def _():
        store_rows(total_ref, y_ref, table_ref, stage_ref, out_ref)


def backward_kernel(count, grad_count, y_ref, *refs):
    rows, grads, refs = refs[:count], refs[count : count + grad_count], refs[count + grad_count :]
    table_ref, gate_ref, up_ref, down_ref, out_ref, rows_ref, grads_ref, total_ref, stage_ref = refs
    real = out_ref.shape[2]

    @pl.when(pl.program_id(0) == 0)
    def _():
        rows_ref[...] = jnp.zeros_like(rows_ref)
        grads_ref[...] = jnp.zeros_like(grads_ref)
        stage_ref[...] = jnp.zeros_like(stage_ref)
        load_rows(rows, y_ref, table_ref, stage_ref, rows_ref, real)
        if grads:
            load_rows(grads, y_ref, table_ref, stage_ref, grads_ref, real)
        else:
            load_rows(rows, y_ref, table_ref, stage_ref, grads_ref, real, real)

    gate = dot_nn(rows_ref[...], gate_ref[...])
    up = dot_nn(rows_ref[...], up_ref[...])
    d_hidden = dot_nt(grads_ref[...], down_ref[...])
    sigmoid = jax.nn.sigmoid(gate)
    d_gate = (d_hidden * up * sigmoid * (1.0 + gate * (1.0 - sigmoid))).astype(jnp.bfloat16)
    d_up = (d_hidden * gate * sigmoid).astype(jnp.bfloat16)
    add_share(total_ref, dot_nt(d_gate, gate_ref[...]) + dot_nt(d_up, up_ref[...]))

    @pl.when(pl.program_id(0) == pl.num_programs(0) - 1)
    def _():
        store_rows(total_ref, y_ref, table_ref, stage_ref, out_ref)


def weight_specs(width, hidden):
    return [
        pl.BlockSpec((width, HIDDEN_BLOCK), lambda j, *_: (0, j)),
        pl.BlockSpec((width, HIDDEN_BLOCK), lambda j, *_: (0, j)),
        pl.BlockSpec((HIDDEN_BLOCK, width), lambda j, *_: (j, 0)),
    ]


def whole(shape):
    return pl.BlockSpec(shape, lambda j, *_: (0,) * len(shape))


def expert_call(kernel, column, rows, grads, grid, table, weights):
    width, hidden = weights[0].shape
    total = COLUMN * GROUP
    backward = kernel is backward_kernel
    inputs = list(rows) + list(grads) + [table]
    counts = (len(rows), len(grads)) if backward else (len(rows),)
    return pl.pallas_call(
        functools.partial(kernel, *counts),
        grid_spec=pltpu.PrefetchScalarGridSpec(
            num_scalar_prefetch=1,
            grid=(hidden // HIDDEN_BLOCK,),
            in_specs=[whole(v.shape) for v in inputs] + weight_specs(width, hidden),
            out_specs=whole(grid),
            scratch_shapes=[pltpu.VMEM((total, width), jnp.bfloat16)] * (2 if backward else 1)
            + [
                pltpu.VMEM((total, width), jnp.float32),
                pltpu.VMEM((PARTS * GROUP, grid[3]), jnp.bfloat16),
            ],
        ),
        out_shape=jax.ShapeDtypeStruct(grid, jnp.bfloat16),
        compiler_params=pltpu.CompilerParams(vmem_limit_bytes=VMEM_LIMIT),
        cost_estimate=pl.CostEstimate(
            flops=(10 if backward else 6) * total * width * hidden,
            bytes_accessed=6 * width * hidden,
            transcendentals=total * hidden,
        ),
        name="expert_backward" if backward else "expert_forward",
    )(column, *inputs, *weights)


def pick_kernel(z_ref, key_ref, *refs):
    blocks, outs, source_ref = refs[:-5], refs[-5:-1], refs[-1]
    lanes = key_ref.shape[1]
    for d, block in enumerate(blocks):
        tokens = block.shape[0]
        place = (z_ref[0] + d) % len(blocks) * tokens
        source_ref[pl.ds(pl.multiple_of(place, tokens), tokens), :] = block[...]
    slots = iota((GROUP, lanes), 0)
    hits = [key_ref[d : d + 1, :] == slots for d in range(len(outs))]
    rows = dot_nn(jnp.concatenate(hits, axis=0).astype(jnp.bfloat16), source_ref[...])
    for d, out in enumerate(outs):
        out[...] = rows[d * GROUP : d * GROUP + out.shape[0]].astype(jnp.bfloat16)


def pair_kernel(z_ref, key_ref, weight_ref, *refs):
    blocks, outs, source_ref = refs[:-5], refs[-5:-1], refs[-1]
    lanes = key_ref.shape[1]
    count = len(blocks) // 2
    slots = iota((GROUP, lanes), 0)
    hits = [key_ref[d : d + 1, :] == slots for d in range(len(outs))]
    real = outs[0].shape[0] // 2
    for stream in range(2):
        for d, block in enumerate(blocks[stream * count : (stream + 1) * count]):
            tokens = block.shape[0]
            place = (z_ref[0] + d) % count * tokens
            source_ref[pl.ds(pl.multiple_of(place, tokens), tokens), :] = block[...]
        if stream:
            table = [jnp.where(hit, weight_ref[d : d + 1, :], 0.0) for d, hit in enumerate(hits)]
            table = jnp.concatenate(table, axis=0)
            high = table.astype(jnp.bfloat16)
            low = (table - high.astype(jnp.float32)).astype(jnp.bfloat16)
            rows = dot_nn(high, source_ref[...]) + dot_nn(low, source_ref[...])
        else:
            rows = dot_nn(jnp.concatenate(hits, axis=0).astype(jnp.bfloat16), source_ref[...])
        for d, out in enumerate(outs):
            out[stream * real : (stream + 1) * real, :] = rows[d * GROUP : d * GROUP + real].astype(jnp.bfloat16)


def column_pick(kernel, at_z, tables, blocks, parts, tokens, real):
    width = blocks[0].shape[1]
    lanes = tables[0].shape[1]
    return pl.pallas_call(
        kernel,
        grid_spec=pltpu.PrefetchScalarGridSpec(
            num_scalar_prefetch=1,
            grid=(1,),
            in_specs=[whole(t.shape) for t in tables]
            + [pl.BlockSpec((tokens, width), lambda j, *_, part=part: (part, 0)) for part in parts],
            out_specs=[whole((real, width))] * 4,
            scratch_shapes=[pltpu.VMEM((lanes, width), jnp.bfloat16)],
        ),
        out_shape=[jax.ShapeDtypeStruct((real, width), jnp.bfloat16)] * 4,
        compiler_params=pltpu.CompilerParams(vmem_limit_bytes=VMEM_LIMIT),
        cost_estimate=pl.CostEstimate(
            flops=8 * GROUP * lanes * width, bytes_accessed=4 * lanes * width, transcendentals=0
        ),
        name="column_pick",
    )(at_z, *tables, *blocks)


def gathered_round(block, axis, cut, gates=None):
    gates = gates or {}
    half = lax.axis_size(axis) // 2
    up, down = block, block
    ahead, behind = [], []
    for r in range(1, half):
        if r in gates:
            up, down = after((up, down), gates[r])
        up, down = turned(up, axis, 1), turned(down, axis, -1)
        ahead.append(down)
        behind.append(up)
    if half in gates:
        up, down = after((up, down), gates[half])
    far = turned(up[:cut], axis, 1), turned(down[cut:], axis, -1)
    return [block] + ahead, far, behind[::-1]


def on_device(
    enter_fwd,
    held_fwd,
    route_fwd,
    prob_fwd,
    enter_grad,
    held_grad,
    saved_inputs,
    route_grad,
    prob_grad,
    norm_gain,
    w_gate,
    w_up,
    w_down,
):
    tokens = held_fwd.shape[1]
    width = held_fwd.shape[2]
    layers_z, layers_y = lax.axis_size("z"), lax.axis_size("y")
    at_z, at_y = lax.axis_index("z"), lax.axis_index("y")
    experts = layers_z * layers_y
    lanes = PARTS * tokens
    chunk = CAP * PARTS
    part = width // PARTS
    gain = norm_gain[0]
    gate_w, up_w, down_w = w_gate[0, 0], w_up[0, 0], w_down[0, 0]
    section = lax.axis_index("pipe")
    last_section = lax.axis_size("pipe") - 1

    def exchanged(chunks):
        return lax.all_to_all(chunks, ("z", "y"), split_axis=0, concat_axis=0, tiled=True)

    spread = (iota((tokens, lanes), 0) == iota((tokens, lanes), 1) % tokens).astype(jnp.bfloat16)
    choices = route_fwd.shape[-1]
    routes = jnp.concatenate([route_fwd[:, 0], route_grad[:, 0]]).transpose(0, 2, 1).astype(jnp.bfloat16)
    probs = jnp.concatenate([prob_fwd[:, 0], prob_grad[:, 0]]).transpose(0, 2, 1)
    earlier = earlier_tokens(lanes, tokens)
    column_owner = at_z * layers_y + (at_y + iota((layers_y, lanes), 0)) % layers_y

    wide_saved, scale_saved, normed_saved = norm_rows(
        saved_inputs[:, 0].reshape(STEPS * tokens, width), gain
    )
    wide, _, normed_fwd = norm_rows(held_fwd[0], gain)
    place = (iota((tokens, lanes), 0) + at_z * tokens == iota((tokens, lanes), 1)).astype(jnp.bfloat16)
    notes = [routes[0], routes[STEPS], routes[STEPS + 1]] + split_three(probs[STEPS])
    fields = len(notes)
    notes = jnp.dot(jnp.concatenate(notes), place, preferred_element_type=jnp.float32).astype(jnp.bfloat16)
    notes = jnp.concatenate(list(notes.reshape(fields, choices, lanes)), axis=1)
    notes = jnp.pad(notes, ((0, choices), (0, width - fields * lanes)))
    payload = jnp.concatenate([normed_saved[:tokens], held_grad[0], notes])
    ahead, far, behind = gathered_round(payload, "z", tokens)
    noted = far[1][tokens : tokens + choices].astype(jnp.float32)
    for block in ahead + behind:
        noted = noted + block[2 * tokens : 2 * tokens + choices].astype(jnp.float32)
    noted = [noted[:, i * lanes : (i + 1) * lanes] for i in range(fields)]

    def column_keys(route, prob):
        route = route.astype(jnp.int32)
        hit = jnp.zeros((layers_y, lanes), jnp.bool_)
        weight = None if prob is None else jnp.zeros((layers_y, lanes), jnp.float32)
        for k in range(choices):
            same = column_owner == route[k][None, :]
            hit = hit | same
            if prob is not None:
                weight = jnp.where(same, prob[k][None, :], weight)
        block = iota((layers_y, lanes), 1) // tokens
        return jnp.where(hit, ranked(hit, earlier) + block * CAP, -1), weight

    forward_keys = column_keys(noted[0], None)
    grad_keys = column_keys(noted[1], noted[3] + noted[4] + noted[5])
    later_keys = column_keys(noted[2], None)

    def column_sent(rows):
        return [rows[0]] + [turned(rows[d], "y", d) for d in range(1, layers_y)]

    row, column = at_z.astype(jnp.int32).reshape(1), at_y.astype(jnp.int32).reshape(1)

    real = layers_z * CAP
    blocks = [ahead + [far[i]] + behind for i in range(2)]
    parts = [[i] * len(ahead) + [0] + [i] * len(behind) for i in range(2)]
    rows_grad = column_pick(
        pair_kernel, row, grad_keys, blocks[0] + blocks[1], parts[0] + parts[1], tokens, 2 * real
    )
    come_pair = column_sent(rows_grad)
    fwd_ahead, fwd_far, fwd_behind = gathered_round(
        after(normed_fwd, rows_grad), "z", tokens // 2, {3: (come_pair[1], come_pair[3]), 4: come_pair[2]}
    )

    saved_gathered = lax.all_gather(after(normed_saved[tokens:], far), "z", axis=0, tiled=True)

    route_lanes = jnp.dot(
        routes.reshape(-1, tokens), spread, preferred_element_type=jnp.float32
    )
    route_lanes = route_lanes.astype(jnp.int32).reshape(2 * STEPS, choices, lanes)
    prob_lanes = jnp.dot(
        probs.reshape(-1, tokens), spread.astype(jnp.float32), precision=lax.Precision.HIGHEST
    )
    prob_lanes = prob_lanes.reshape(2 * STEPS, choices, lanes)

    def forward_send(block, step):
        wide, _, normed = norm_rows(block, gain)
        key, _ = slot_keys(route_lanes[step], prob_lanes[step], experts, tokens, earlier)
        send = picked(select_table(key, chunk), to_parts(normed)).astype(jnp.bfloat16)
        return wide, send.reshape(experts, chunk, part)

    def forward_mixing(step):
        key, weight = slot_keys(route_lanes[step], prob_lanes[step], experts, tokens, earlier)
        return tuple(t.T for t in weight_table(key, weight, chunk))

    def grad_send(block, step):
        key, weight = slot_keys(
            route_lanes[STEPS + step], prob_lanes[STEPS + step], experts, tokens, earlier
        )
        high, low = weight_table(key, weight, chunk)
        parts = to_parts(block)
        send = (picked(high, parts) + picked(low, parts)).astype(jnp.bfloat16)
        return send.reshape(experts, chunk, part)

    def grad_select(step):
        key, _ = slot_keys(
            route_lanes[STEPS + step], prob_lanes[STEPS + step], experts, tokens, earlier
        )
        return select_table(key, chunk).T

    def forward_out(wide, mixing, back):
        high, low = mixing
        back = back.reshape(experts * chunk, part)
        return (wide + from_parts(picked(high, back) + picked(low, back), tokens)).astype(jnp.bfloat16)

    def grad_out(block, select, step, back):
        d_normed = from_parts(picked(select, back.reshape(experts * chunk, part)), tokens)
        mine = slice(step * tokens, (step + 1) * tokens)
        wide, scale = wide_saved[mine], scale_saved[mine]
        scaled_u = d_normed * gain[None, :]
        inner = jnp.mean(scaled_u * wide, axis=-1, keepdims=True)
        d_block = scale * scaled_u - wide * (scale * scale * scale) * inner
        return (block.astype(jnp.float32) + d_block).astype(jnp.bfloat16)

    table = regroup(PARTS, layers_z * CAP, GROUP)
    weights = (gate_w, up_w, down_w)
    grid = (layers_z, layers_y, chunk, part)
    flat = (experts, chunk, part)
    block_grad = held_grad[0]
    outputs_all, grads_all = [], []
    blocks = fwd_ahead + [jnp.concatenate(fwd_far)] + fwd_behind
    come_fwd = column_sent(
        column_pick(pick_kernel, row, [after(forward_keys[0], come_pair)], blocks, [0] * len(blocks), tokens, real)
    )
    result_grad = expert_call(backward_kernel, column, come_pair, [], grid, table, weights)
    mixing, select = forward_mixing(0), grad_select(0)
    ready = (come_fwd, saved_gathered)
    for step in range(STEPS):
        more = step + 1 < STEPS
        back_grad = exchanged(after(result_grad.reshape(flat), *ready))
        result_fwd = expert_call(forward_kernel, column, come_fwd, [], grid, table, weights)
        if more:
            rows_saved = column_pick(
                pick_kernel,
                jnp.zeros_like(row),
                [after(later_keys[0], come_fwd)],
                [saved_gathered],
                [0],
                lanes,
                real,
            )
            come_saved = column_sent(rows_saved)
        back_fwd = exchanged(after(result_fwd.reshape(flat), back_grad, come_saved))
        out_grad = grad_out(block_grad, select, step, back_grad)
        grads_all.append(out_grad[None])
        if more:
            moved_grad = passed_along(out_grad, "pipe", -1)
            block_grad = jnp.where(section == last_section, enter_grad[step], moved_grad)
            send_grad = grad_send(block_grad, step + 1)
            back_fwd, send_grad = lax.optimization_barrier((back_fwd, send_grad))
            come_grad = exchanged(send_grad)
        out_fwd = forward_out(wide, mixing, back_fwd)
        outputs_all.append(out_fwd[None])
        if more:
            moved_fwd = passed_along(out_fwd, "pipe", 1)
            block_fwd = jnp.where(section == 0, enter_fwd[step], moved_fwd)
            wide, send_fwd = forward_send(block_fwd, step + 1)
            mixing, select = forward_mixing(step + 1), grad_select(step + 1)
            come_fwd = [exchanged(after(send_fwd, come_grad)).reshape(grid)]
            result_grad = expert_call(
                backward_kernel, column, come_saved, [come_grad.reshape(grid)], grid, table, weights
            )
            ready = (come_fwd,)
    return (jnp.stack(outputs_all), jnp.stack(grads_all))


def solution(mesh):
    sections, owners = mesh.devices.shape
    grid = Mesh(mesh.devices.reshape(sections, owners // COLUMN, COLUMN), ("pipe", "z", "y"))
    expert = ("z", "y")
    return jax.shard_map(
        on_device,
        mesh=grid,
        in_specs=(
            P(None, expert, None),
            P("pipe", expert, None),
            P(None, "pipe", expert, None),
            P(None, "pipe", expert, None),
            P(None, expert, None),
            P("pipe", expert, None),
            P(None, "pipe", expert, None),
            P(None, "pipe", expert, None),
            P(None, "pipe", expert, None),
            P("pipe", None),
            P("pipe", expert, None, None),
            P("pipe", expert, None, None),
            P("pipe", expert, None, None),
        ),
        out_specs=(P(None, "pipe", expert, None), P(None, "pipe", expert, None)),
        check_vma=False,
    )
```

```python
import functools

import jax
import jax.numpy as jnp
from jax import lax
from jax.experimental import pallas as pl
from jax.experimental.pallas import tpu as pltpu
from jax.sharding import Mesh, PartitionSpec as P

STEPS = 2
CAP = 9
PARTS = 8
COLUMN = 4
GROUP = 80
HIDDEN_BLOCK = 384
VMEM_LIMIT = 58 * 1024 * 1024


epsilon = 1e-06


def passed_along(block, axis, distance):
    devices = range(lax.axis_size(axis))
    route = [(i - distance, i) for i in devices if i - distance in devices]
    return lax.ppermute(block, axis, route)


def turned(block, axis, distance):
    size = lax.axis_size(axis)
    return lax.ppermute(block, axis, [(i, (i + distance) % size) for i in range(size)])


def after(value, *earlier):
    return lax.optimization_barrier((value,) + earlier)[0]


def norm_rows(block, gain):
    wide = block.astype(jnp.float32)
    scale = lax.rsqrt(jnp.mean(wide * wide, axis=-1, keepdims=True) + epsilon)
    normed = (wide * scale * gain[None, :]).astype(jnp.bfloat16)
    return (wide, scale, normed)


def split_two(values):
    high = lax.reduce_precision(values, exponent_bits=8, mantissa_bits=7)
    return high.astype(jnp.bfloat16), (values - high).astype(jnp.bfloat16)


def split_three(values):
    high = lax.reduce_precision(values, exponent_bits=8, mantissa_bits=7)
    middle = lax.reduce_precision(values - high, exponent_bits=8, mantissa_bits=7)
    return [t.astype(jnp.bfloat16) for t in (high, middle, values - high - middle)]


def iota(shape, axis):
    return lax.broadcasted_iota(jnp.int32, shape, axis)


def earlier_tokens(lanes, tokens):
    before, now = iota((lanes, lanes), 0), iota((lanes, lanes), 1)
    return ((before // tokens == now // tokens) & (before < now)).astype(jnp.bfloat16)


def ranked(hit, earlier):
    return jnp.dot(hit.astype(jnp.bfloat16), earlier, preferred_element_type=jnp.float32).astype(jnp.int32)


def slot_keys(route_lanes, prob_lanes, experts, tokens, earlier):
    lanes = route_lanes.shape[1]
    names = iota((experts, lanes), 0)
    hit = jnp.zeros((experts, lanes), jnp.bool_)
    weight = jnp.zeros((experts, lanes), jnp.float32)
    for k in range(route_lanes.shape[0]):
        same = names == route_lanes[k][None, :]
        hit = hit | same
        weight = jnp.where(same, prob_lanes[k][None, :], weight)
    part = iota((experts, lanes), 1) // tokens
    return jnp.where(hit, ranked(hit, earlier) * PARTS + part, -1), weight


def select_table(key, rows):
    hits = key[:, None, :] == iota((key.shape[0], rows, key.shape[1]), 1)
    return hits.astype(jnp.bfloat16).reshape(-1, key.shape[1])


def weight_table(key, weight, rows):
    hits = key[:, None, :] == iota((key.shape[0], rows, key.shape[1]), 1)
    return split_two(jnp.where(hits, weight[:, None, :], 0.0).reshape(-1, key.shape[1]))


def to_parts(block):
    tokens, width = block.shape
    return block.reshape(tokens, PARTS, width // PARTS).transpose(1, 0, 2).reshape(PARTS * tokens, -1)


def from_parts(block, tokens):
    return block.reshape(PARTS, tokens, -1).transpose(1, 0, 2).reshape(tokens, -1)


def picked(table, block):
    return jnp.dot(table, block, preferred_element_type=jnp.float32)


def dot_nn(a, b):
    return jnp.dot(a, b, preferred_element_type=jnp.float32)


def dot_nt(a, b):
    return lax.dot_general(a, b, (((1,), (1,)), ((), ())), preferred_element_type=jnp.float32)


def regroup(parts, rows, group):
    size = parts * group
    to, come = iota((size, size), 0), iota((size, size), 1)
    part, row = to // group, to % group
    source, place = come // group, come % group
    same = (source == row // CAP) & (place == (row % CAP) * parts + part) & (row < rows)
    return same.astype(jnp.bfloat16)


def rows_from_chunks(chunks_ref, column, table_ref, stage_ref, rows_ref, at):
    layers_z, _, real, part = chunks_ref.shape
    for z in range(layers_z):
        stage_ref[z * GROUP : z * GROUP + real, :] = chunks_ref[z, column]
    placed = dot_nn(table_ref[...], stage_ref[...]).astype(jnp.bfloat16)
    for c in range(PARTS):
        rows_ref[at : at + GROUP, c * part : (c + 1) * part] = placed[c * GROUP : (c + 1) * GROUP]


def rows_to_chunks(total_ref, at, table_ref, stage_ref, out_ref, column):
    layers_z, _, real, part = out_ref.shape
    for c in range(PARTS):
        stage_ref[c * GROUP : (c + 1) * GROUP, :] = total_ref[
            at : at + GROUP, c * part : (c + 1) * part
        ].astype(jnp.bfloat16)
    placed = lax.dot_general(
        table_ref[...], stage_ref[...], (((0,), (0,)), ((), ())), preferred_element_type=jnp.float32
    ).astype(jnp.bfloat16)
    for z in range(layers_z):
        out_ref[z, column] = placed[z * GROUP : z * GROUP + real]


def add_share(total_ref, share):
    @pl.when(pl.program_id(0) == 0)
    def _():
        total_ref[...] = share

    @pl.when(pl.program_id(0) > 0)
    def _():
        total_ref[...] += share


def load_rows(refs, y_ref, table_ref, stage_ref, rows_ref, real, at=0):
    for d in range(COLUMN):
        if len(refs) > 1:
            rows_ref[d * GROUP : d * GROUP + real, :] = refs[d][at : at + real, :]
        else:
            column = (y_ref[0] + COLUMN - d) % COLUMN
            rows_from_chunks(refs[0], column, table_ref, stage_ref, rows_ref, d * GROUP)


def store_rows(total_ref, y_ref, table_ref, stage_ref, out_ref):
    for d in range(COLUMN):
        column = (y_ref[0] + COLUMN - d) % COLUMN
        rows_to_chunks(total_ref, d * GROUP, table_ref, stage_ref, out_ref, column)


def forward_kernel(count, y_ref, *refs):
    rows, refs = refs[:count], refs[count:]
    table_ref, gate_ref, up_ref, down_ref, out_ref, rows_ref, total_ref, stage_ref = refs

    @pl.when(pl.program_id(0) == 0)
    def _():
        rows_ref[...] = jnp.zeros_like(rows_ref)
        stage_ref[...] = jnp.zeros_like(stage_ref)
        load_rows(rows, y_ref, table_ref, stage_ref, rows_ref, out_ref.shape[2])

    gate = dot_nn(rows_ref[...], gate_ref[...])
    up = dot_nn(rows_ref[...], up_ref[...])
    hidden = (gate * jax.nn.sigmoid(gate) * up).astype(jnp.bfloat16)
    add_share(total_ref, dot_nn(hidden, down_ref[...]))

    @pl.when(pl.program_id(0) == pl.num_programs(0) - 1)
    def _():
        store_rows(total_ref, y_ref, table_ref, stage_ref, out_ref)


def backward_kernel(count, grad_count, y_ref, *refs):
    rows, grads, refs = refs[:count], refs[count : count + grad_count], refs[count + grad_count :]
    table_ref, gate_ref, up_ref, down_ref, out_ref, rows_ref, grads_ref, total_ref, stage_ref = refs
    real = out_ref.shape[2]

    @pl.when(pl.program_id(0) == 0)
    def _():
        rows_ref[...] = jnp.zeros_like(rows_ref)
        grads_ref[...] = jnp.zeros_like(grads_ref)
        stage_ref[...] = jnp.zeros_like(stage_ref)
        load_rows(rows, y_ref, table_ref, stage_ref, rows_ref, real)
        if grads:
            load_rows(grads, y_ref, table_ref, stage_ref, grads_ref, real)
        else:
            load_rows(rows, y_ref, table_ref, stage_ref, grads_ref, real, real)

    gate = dot_nn(rows_ref[...], gate_ref[...])
    up = dot_nn(rows_ref[...], up_ref[...])
    d_hidden = dot_nt(grads_ref[...], down_ref[...])
    sigmoid = jax.nn.sigmoid(gate)
    d_gate = (d_hidden * up * sigmoid * (1.0 + gate * (1.0 - sigmoid))).astype(jnp.bfloat16)
    d_up = (d_hidden * gate * sigmoid).astype(jnp.bfloat16)
    add_share(total_ref, dot_nt(d_gate, gate_ref[...]) + dot_nt(d_up, up_ref[...]))

    @pl.when(pl.program_id(0) == pl.num_programs(0) - 1)
    def _():
        store_rows(total_ref, y_ref, table_ref, stage_ref, out_ref)


def weight_specs(width, hidden):
    return [
        pl.BlockSpec((width, HIDDEN_BLOCK), lambda j, *_: (0, j)),
        pl.BlockSpec((width, HIDDEN_BLOCK), lambda j, *_: (0, j)),
        pl.BlockSpec((HIDDEN_BLOCK, width), lambda j, *_: (j, 0)),
    ]


def whole(shape):
    return pl.BlockSpec(shape, lambda j, *_: (0,) * len(shape))


def expert_call(kernel, column, rows, grads, grid, table, weights):
    width, hidden = weights[0].shape
    total = COLUMN * GROUP
    backward = kernel is backward_kernel
    inputs = list(rows) + list(grads) + [table]
    counts = (len(rows), len(grads)) if backward else (len(rows),)
    return pl.pallas_call(
        functools.partial(kernel, *counts),
        grid_spec=pltpu.PrefetchScalarGridSpec(
            num_scalar_prefetch=1,
            grid=(hidden // HIDDEN_BLOCK,),
            in_specs=[whole(v.shape) for v in inputs] + weight_specs(width, hidden),
            out_specs=whole(grid),
            scratch_shapes=[pltpu.VMEM((total, width), jnp.bfloat16)] * (2 if backward else 1)
            + [
                pltpu.VMEM((total, width), jnp.float32),
                pltpu.VMEM((PARTS * GROUP, grid[3]), jnp.bfloat16),
            ],
        ),
        out_shape=jax.ShapeDtypeStruct(grid, jnp.bfloat16),
        compiler_params=pltpu.CompilerParams(vmem_limit_bytes=VMEM_LIMIT),
        cost_estimate=pl.CostEstimate(
            flops=(10 if backward else 6) * total * width * hidden,
            bytes_accessed=6 * width * hidden,
            transcendentals=total * hidden,
        ),
        name="expert_backward" if backward else "expert_forward",
    )(column, *inputs, *weights)


def pick_kernel(z_ref, key_ref, *refs):
    blocks, outs, source_ref = refs[:-5], refs[-5:-1], refs[-1]
    lanes = key_ref.shape[1]
    for d, block in enumerate(blocks):
        tokens = block.shape[0]
        place = (z_ref[0] + d) % len(blocks) * tokens
        source_ref[pl.ds(pl.multiple_of(place, tokens), tokens), :] = block[...]
    slots = iota((GROUP, lanes), 0)
    hits = [key_ref[d : d + 1, :] == slots for d in range(len(outs))]
    rows = dot_nn(jnp.concatenate(hits, axis=0).astype(jnp.bfloat16), source_ref[...])
    for d, out in enumerate(outs):
        out[...] = rows[d * GROUP : d * GROUP + out.shape[0]].astype(jnp.bfloat16)


def pair_kernel(z_ref, key_ref, weight_ref, *refs):
    blocks, outs, source_ref = refs[:-5], refs[-5:-1], refs[-1]
    lanes = key_ref.shape[1]
    count = len(blocks) // 2
    slots = iota((GROUP, lanes), 0)
    hits = [key_ref[d : d + 1, :] == slots for d in range(len(outs))]
    real = outs[0].shape[0] // 2
    for stream in range(2):
        for d, block in enumerate(blocks[stream * count : (stream + 1) * count]):
            tokens = block.shape[0]
            place = (z_ref[0] + d) % count * tokens
            source_ref[pl.ds(pl.multiple_of(place, tokens), tokens), :] = block[...]
        if stream:
            table = [jnp.where(hit, weight_ref[d : d + 1, :], 0.0) for d, hit in enumerate(hits)]
            table = jnp.concatenate(table, axis=0)
            high = table.astype(jnp.bfloat16)
            low = (table - high.astype(jnp.float32)).astype(jnp.bfloat16)
            rows = dot_nn(high, source_ref[...]) + dot_nn(low, source_ref[...])
        else:
            rows = dot_nn(jnp.concatenate(hits, axis=0).astype(jnp.bfloat16), source_ref[...])
        for d, out in enumerate(outs):
            out[stream * real : (stream + 1) * real, :] = rows[d * GROUP : d * GROUP + real].astype(jnp.bfloat16)


def column_pick(kernel, at_z, tables, blocks, parts, tokens, real):
    width = blocks[0].shape[1]
    lanes = tables[0].shape[1]
    return pl.pallas_call(
        kernel,
        grid_spec=pltpu.PrefetchScalarGridSpec(
            num_scalar_prefetch=1,
            grid=(1,),
            in_specs=[whole(t.shape) for t in tables]
            + [pl.BlockSpec((tokens, width), lambda j, *_, part=part: (part, 0)) for part in parts],
            out_specs=[whole((real, width))] * 4,
            scratch_shapes=[pltpu.VMEM((lanes, width), jnp.bfloat16)],
        ),
        out_shape=[jax.ShapeDtypeStruct((real, width), jnp.bfloat16)] * 4,
        compiler_params=pltpu.CompilerParams(vmem_limit_bytes=VMEM_LIMIT),
        cost_estimate=pl.CostEstimate(
            flops=8 * GROUP * lanes * width, bytes_accessed=4 * lanes * width, transcendentals=0
        ),
        name="column_pick",
    )(at_z, *tables, *blocks)


def gathered_round(block, axis, cut, gates=None):
    gates = gates or {}
    half = lax.axis_size(axis) // 2
    up, down = block, block
    ahead, behind = [], []
    for r in range(1, half):
        if r in gates:
            up, down = after((up, down), gates[r])
        up, down = turned(up, axis, 1), turned(down, axis, -1)
        ahead.append(down)
        behind.append(up)
    if half in gates:
        up, down = after((up, down), gates[half])
    far = turned(up[:cut], axis, 1), turned(down[cut:], axis, -1)
    return [block] + ahead, far, behind[::-1]


def on_device(
    enter_fwd,
    held_fwd,
    route_fwd,
    prob_fwd,
    enter_grad,
    held_grad,
    saved_inputs,
    route_grad,
    prob_grad,
    norm_gain,
    w_gate,
    w_up,
    w_down,
):
    tokens = held_fwd.shape[1]
    width = held_fwd.shape[2]
    layers_z, layers_y = lax.axis_size("z"), lax.axis_size("y")
    at_z, at_y = lax.axis_index("z"), lax.axis_index("y")
    experts = layers_z * layers_y
    lanes = PARTS * tokens
    chunk = CAP * PARTS
    part = width // PARTS
    gain = norm_gain[0]
    gate_w, up_w, down_w = w_gate[0, 0], w_up[0, 0], w_down[0, 0]
    section = lax.axis_index("pipe")
    last_section = lax.axis_size("pipe") - 1

    def exchanged(chunks):
        return lax.all_to_all(chunks, ("z", "y"), split_axis=0, concat_axis=0, tiled=True)

    spread = (iota((tokens, lanes), 0) == iota((tokens, lanes), 1) % tokens).astype(jnp.bfloat16)
    choices = route_fwd.shape[-1]
    routes = jnp.concatenate([route_fwd[:, 0], route_grad[:, 0]]).transpose(0, 2, 1).astype(jnp.bfloat16)
    probs = jnp.concatenate([prob_fwd[:, 0], prob_grad[:, 0]]).transpose(0, 2, 1)
    earlier = earlier_tokens(lanes, tokens)
    column_owner = at_z * layers_y + (at_y + iota((layers_y, lanes), 0)) % layers_y

    wide_saved, scale_saved, normed_saved = norm_rows(
        saved_inputs[:, 0].reshape(STEPS * tokens, width), gain
    )
    wide, _, normed_fwd = norm_rows(held_fwd[0], gain)
    place = (iota((tokens, lanes), 0) + at_z * tokens == iota((tokens, lanes), 1)).astype(jnp.bfloat16)
    notes = [routes[0], routes[STEPS], routes[STEPS + 1]] + split_three(probs[STEPS])
    fields = len(notes)
    notes = jnp.dot(jnp.concatenate(notes), place, preferred_element_type=jnp.float32).astype(jnp.bfloat16)
    notes = jnp.concatenate(list(notes.reshape(fields, choices, lanes)), axis=1)
    notes = jnp.pad(notes, ((0, 0), (0, width - fields * lanes)))
    payload = jnp.concatenate([normed_saved[:tokens], held_grad[0], notes])
    ahead, far, behind = gathered_round(payload, "z", tokens)
    noted = far[1][tokens : tokens + choices].astype(jnp.float32)
    for block in ahead + behind:
        noted = noted + block[2 * tokens : 2 * tokens + choices].astype(jnp.float32)
    noted = [noted[:, i * lanes : (i + 1) * lanes] for i in range(fields)]

    def column_keys(route, prob):
        route = route.astype(jnp.int32)
        hit = jnp.zeros((layers_y, lanes), jnp.bool_)
        weight = None if prob is None else jnp.zeros((layers_y, lanes), jnp.float32)
        for k in range(choices):
            same = column_owner == route[k][None, :]
            hit = hit | same
            if prob is not None:
                weight = jnp.where(same, prob[k][None, :], weight)
        block = iota((layers_y, lanes), 1) // tokens
        return jnp.where(hit, ranked(hit, earlier) + block * CAP, -1), weight

    forward_keys = column_keys(noted[0], None)
    grad_keys = column_keys(noted[1], noted[3] + noted[4] + noted[5])
    later_keys = column_keys(noted[2], None)

    def column_sent(rows):
        return [rows[0]] + [turned(rows[d], "y", d) for d in range(1, layers_y)]

    row, column = at_z.astype(jnp.int32).reshape(1), at_y.astype(jnp.int32).reshape(1)

    real = layers_z * CAP
    blocks = [ahead + [far[i]] + behind for i in range(2)]
    parts = [[i] * len(ahead) + [0] + [i] * len(behind) for i in range(2)]
    rows_grad = column_pick(
        pair_kernel, row, grad_keys, blocks[0] + blocks[1], parts[0] + parts[1], tokens, 2 * real
    )
    come_pair = column_sent(rows_grad)
    fwd_ahead, fwd_far, fwd_behind = gathered_round(
        after(normed_fwd, rows_grad), "z", tokens // 2, {3: (come_pair[1], come_pair[3]), 4: come_pair[2]}
    )

    saved_gathered = lax.all_gather(after(normed_saved[tokens:], far), "z", axis=0, tiled=True)

    route_lanes = jnp.dot(
        routes.reshape(-1, tokens), spread, preferred_element_type=jnp.float32
    )
    route_lanes = route_lanes.astype(jnp.int32).reshape(2 * STEPS, choices, lanes)
    prob_lanes = jnp.dot(
        probs.reshape(-1, tokens), spread.astype(jnp.float32), precision=lax.Precision.HIGHEST
    )
    prob_lanes = prob_lanes.reshape(2 * STEPS, choices, lanes)

    def forward_send(block, step):
        wide, _, normed = norm_rows(block, gain)
        key, _ = slot_keys(route_lanes[step], prob_lanes[step], experts, tokens, earlier)
        send = picked(select_table(key, chunk), to_parts(normed)).astype(jnp.bfloat16)
        return wide, send.reshape(experts, chunk, part)

    def forward_mixing(step):
        key, weight = slot_keys(route_lanes[step], prob_lanes[step], experts, tokens, earlier)
        return tuple(t.T for t in weight_table(key, weight, chunk))

    def grad_send(block, step):
        key, weight = slot_keys(
            route_lanes[STEPS + step], prob_lanes[STEPS + step], experts, tokens, earlier
        )
        high, low = weight_table(key, weight, chunk)
        parts = to_parts(block)
        send = (picked(high, parts) + picked(low, parts)).astype(jnp.bfloat16)
        return send.reshape(experts, chunk, part)

    def grad_select(step):
        key, _ = slot_keys(
            route_lanes[STEPS + step], prob_lanes[STEPS + step], experts, tokens, earlier
        )
        return select_table(key, chunk).T

    def forward_out(wide, mixing, back):
        high, low = mixing
        back = back.reshape(experts * chunk, part)
        return (wide + from_parts(picked(high, back) + picked(low, back), tokens)).astype(jnp.bfloat16)

    def grad_out(block, select, step, back):
        d_normed = from_parts(picked(select, back.reshape(experts * chunk, part)), tokens)
        mine = slice(step * tokens, (step + 1) * tokens)
        wide, scale = wide_saved[mine], scale_saved[mine]
        scaled_u = d_normed * gain[None, :]
        inner = jnp.mean(scaled_u * wide, axis=-1, keepdims=True)
        d_block = scale * scaled_u - wide * (scale * scale * scale) * inner
        return (block.astype(jnp.float32) + d_block).astype(jnp.bfloat16)

    table = regroup(PARTS, layers_z * CAP, GROUP)
    weights = (gate_w, up_w, down_w)
    grid = (layers_z, layers_y, chunk, part)
    flat = (experts, chunk, part)
    block_grad = held_grad[0]
    outputs_all, grads_all = [], []
    blocks = fwd_ahead + [jnp.concatenate(fwd_far)] + fwd_behind
    come_fwd = column_sent(
        column_pick(pick_kernel, row, [after(forward_keys[0], come_pair)], blocks, [0] * len(blocks), tokens, real)
    )
    result_grad = expert_call(backward_kernel, column, come_pair, [], grid, table, weights)
    mixing, select = forward_mixing(0), grad_select(0)
    ready = (come_fwd, saved_gathered)
    for step in range(STEPS):
        more = step + 1 < STEPS
        back_grad = exchanged(after(result_grad.reshape(flat), *ready))
        result_fwd = expert_call(forward_kernel, column, come_fwd, [], grid, table, weights)
        if more:
            rows_saved = column_pick(
                pick_kernel,
                jnp.zeros_like(row),
                [after(later_keys[0], come_fwd)],
                [saved_gathered],
                [0],
                lanes,
                real,
            )
            come_saved = column_sent(rows_saved)
        back_fwd = exchanged(after(result_fwd.reshape(flat), back_grad, come_saved))
        out_grad = grad_out(block_grad, select, step, back_grad)
        grads_all.append(out_grad[None])
        if more:
            moved_grad = passed_along(out_grad, "pipe", -1)
            block_grad = jnp.where(section == last_section, enter_grad[step], moved_grad)
            send_grad = grad_send(block_grad, step + 1)
            back_fwd, send_grad = lax.optimization_barrier((back_fwd, send_grad))
            come_grad = exchanged(send_grad)
        out_fwd = forward_out(wide, mixing, back_fwd)
        outputs_all.append(out_fwd[None])
        if more:
            moved_fwd = passed_along(out_fwd, "pipe", 1)
            block_fwd = jnp.where(section == 0, enter_fwd[step], moved_fwd)
            wide, send_fwd = forward_send(block_fwd, step + 1)
            mixing, select = forward_mixing(step + 1), grad_select(step + 1)
            come_fwd = [exchanged(after(send_fwd, come_grad)).reshape(grid)]
            result_grad = expert_call(
                backward_kernel, column, come_saved, [come_grad.reshape(grid)], grid, table, weights
            )
            ready = (come_fwd,)
    return (jnp.stack(outputs_all), jnp.stack(grads_all))


def solution(mesh):
    sections, owners = mesh.devices.shape
    grid = Mesh(mesh.devices.reshape(sections, owners // COLUMN, COLUMN), ("pipe", "z", "y"))
    expert = ("z", "y")
    return jax.shard_map(
        on_device,
        mesh=grid,
        in_specs=(
            P(None, expert, None),
            P("pipe", expert, None),
            P(None, "pipe", expert, None),
            P(None, "pipe", expert, None),
            P(None, expert, None),
            P("pipe", expert, None),
            P(None, "pipe", expert, None),
            P(None, "pipe", expert, None),
            P(None, "pipe", expert, None),
            P("pipe", None),
            P("pipe", expert, None, None),
            P("pipe", expert, None, None),
            P("pipe", expert, None, None),
        ),
        out_specs=(P(None, "pipe", expert, None), P(None, "pipe", expert, None)),
        check_vma=False,
    )
```

```python
import functools

import jax
import jax.numpy as jnp
from jax import lax
from jax.experimental import pallas as pl
from jax.experimental.pallas import tpu as pltpu
from jax.sharding import Mesh, PartitionSpec as P

STEPS = 2
CAP = 9
PARTS = 8
COLUMN = 4
GROUP = 80
HIDDEN_BLOCK = 384
VMEM_LIMIT = 58 * 1024 * 1024


epsilon = 1e-06


def passed_along(block, axis, distance):
    devices = range(lax.axis_size(axis))
    route = [(i - distance, i) for i in devices if i - distance in devices]
    return lax.ppermute(block, axis, route)


def turned(block, axis, distance):
    size = lax.axis_size(axis)
    return lax.ppermute(block, axis, [(i, (i + distance) % size) for i in range(size)])


def after(value, *earlier):
    return lax.optimization_barrier((value,) + earlier)[0]


def norm_rows(block, gain):
    wide = block.astype(jnp.float32)
    scale = lax.rsqrt(jnp.mean(wide * wide, axis=-1, keepdims=True) + epsilon)
    normed = (wide * scale * gain[None, :]).astype(jnp.bfloat16)
    return (wide, scale, normed)


def split_two(values):
    high = lax.reduce_precision(values, exponent_bits=8, mantissa_bits=7)
    return high.astype(jnp.bfloat16), (values - high).astype(jnp.bfloat16)


def split_three(values):
    high = lax.reduce_precision(values, exponent_bits=8, mantissa_bits=7)
    middle = lax.reduce_precision(values - high, exponent_bits=8, mantissa_bits=7)
    return [t.astype(jnp.bfloat16) for t in (high, middle, values - high - middle)]


def iota(shape, axis):
    return lax.broadcasted_iota(jnp.int32, shape, axis)


def earlier_tokens(lanes, tokens):
    before, now = iota((lanes, lanes), 0), iota((lanes, lanes), 1)
    return ((before // tokens == now // tokens) & (before < now)).astype(jnp.bfloat16)


def ranked(hit, earlier):
    return jnp.dot(hit.astype(jnp.bfloat16), earlier, preferred_element_type=jnp.float32).astype(jnp.int32)


def slot_keys(route_lanes, prob_lanes, experts, tokens, earlier):
    lanes = route_lanes.shape[1]
    names = iota((experts, lanes), 0)
    hit = jnp.zeros((experts, lanes), jnp.bool_)
    weight = jnp.zeros((experts, lanes), jnp.float32)
    for k in range(route_lanes.shape[0]):
        same = names == route_lanes[k][None, :]
        hit = hit | same
        weight = jnp.where(same, prob_lanes[k][None, :], weight)
    part = iota((experts, lanes), 1) // tokens
    return jnp.where(hit, ranked(hit, earlier) * PARTS + part, -1), weight


def select_table(key, rows):
    hits = key[:, None, :] == iota((key.shape[0], rows, key.shape[1]), 1)
    return hits.astype(jnp.bfloat16).reshape(-1, key.shape[1])


def weight_table(key, weight, rows):
    hits = key[:, None, :] == iota((key.shape[0], rows, key.shape[1]), 1)
    return split_two(jnp.where(hits, weight[:, None, :], 0.0).reshape(-1, key.shape[1]))


def to_parts(block):
    tokens, width = block.shape
    return block.reshape(tokens, PARTS, width // PARTS).transpose(1, 0, 2).reshape(PARTS * tokens, -1)


def from_parts(block, tokens):
    return block.reshape(PARTS, tokens, -1).transpose(1, 0, 2).reshape(tokens, -1)


def picked(table, block):
    return jnp.dot(table, block, preferred_element_type=jnp.float32)


def dot_nn(a, b):
    return jnp.dot(a, b, preferred_element_type=jnp.float32)


def dot_nt(a, b):
    return lax.dot_general(a, b, (((1,), (1,)), ((), ())), preferred_element_type=jnp.float32)


def regroup(parts, rows, group):
    size = parts * group
    to, come = iota((size, size), 0), iota((size, size), 1)
    part, row = to // group, to % group
    source, place = come // group, come % group
    same = (source == row // CAP) & (place == (row % CAP) * parts + part) & (row < rows)
    return same.astype(jnp.bfloat16)


def rows_from_chunks(chunks_ref, column, table_ref, stage_ref, rows_ref, at):
    layers_z, _, real, part = chunks_ref.shape
    for z in range(layers_z):
        stage_ref[z * GROUP : z * GROUP + real, :] = chunks_ref[z, column]
    placed = dot_nn(table_ref[...], stage_ref[...]).astype(jnp.bfloat16)
    for c in range(PARTS):
        rows_ref[at : at + GROUP, c * part : (c + 1) * part] = placed[c * GROUP : (c + 1) * GROUP]


def rows_to_chunks(total_ref, at, table_ref, stage_ref, out_ref, column):
    layers_z, _, real, part = out_ref.shape
    for c in range(PARTS):
        stage_ref[c * GROUP : (c + 1) * GROUP, :] = total_ref[
            at : at + GROUP, c * part : (c + 1) * part
        ].astype(jnp.bfloat16)
    placed = lax.dot_general(
        table_ref[...], stage_ref[...], (((0,), (0,)), ((), ())), preferred_element_type=jnp.float32
    ).astype(jnp.bfloat16)
    for z in range(layers_z):
        out_ref[z, column] = placed[z * GROUP : z * GROUP + real]


def add_share(total_ref, share):
    @pl.when(pl.program_id(0) == 0)
    def _():
        total_ref[...] = share

    @pl.when(pl.program_id(0) > 0)
    def _():
        total_ref[...] += share


def load_rows(refs, y_ref, table_ref, stage_ref, rows_ref, real, at=0):
    for d in range(COLUMN):
        if len(refs) > 1:
            rows_ref[d * GROUP : d * GROUP + real, :] = refs[d][at : at + real, :]
        else:
            column = (y_ref[0] + COLUMN - d) % COLUMN
            rows_from_chunks(refs[0], column, table_ref, stage_ref, rows_ref, d * GROUP)


def store_rows(total_ref, y_ref, table_ref, stage_ref, out_ref):
    for d in range(COLUMN):
        column = (y_ref[0] + COLUMN - d) % COLUMN
        rows_to_chunks(total_ref, d * GROUP, table_ref, stage_ref, out_ref, column)


def forward_kernel(count, y_ref, *refs):
    rows, refs = refs[:count], refs[count:]
    table_ref, gate_ref, up_ref, down_ref, out_ref, rows_ref, total_ref, stage_ref = refs

    @pl.when(pl.program_id(0) == 0)
    def _():
        rows_ref[...] = jnp.zeros_like(rows_ref)
        stage_ref[...] = jnp.zeros_like(stage_ref)
        load_rows(rows, y_ref, table_ref, stage_ref, rows_ref, out_ref.shape[2])

    gate = dot_nn(rows_ref[...], gate_ref[...])
    up = dot_nn(rows_ref[...], up_ref[...])
    hidden = (gate * jax.nn.sigmoid(gate) * up).astype(jnp.bfloat16)
    add_share(total_ref, dot_nn(hidden, down_ref[...]))

    @pl.when(pl.program_id(0) == pl.num_programs(0) - 1)
    def _():
        store_rows(total_ref, y_ref, table_ref, stage_ref, out_ref)


def backward_kernel(count, grad_count, y_ref, *refs):
    rows, grads, refs = refs[:count], refs[count : count + grad_count], refs[count + grad_count :]
    table_ref, gate_ref, up_ref, down_ref, out_ref, rows_ref, grads_ref, total_ref, stage_ref = refs
    real = out_ref.shape[2]

    @pl.when(pl.program_id(0) == 0)
    def _():
        rows_ref[...] = jnp.zeros_like(rows_ref)
        grads_ref[...] = jnp.zeros_like(grads_ref)
        stage_ref[...] = jnp.zeros_like(stage_ref)
        load_rows(rows, y_ref, table_ref, stage_ref, rows_ref, real)
        if grads:
            load_rows(grads, y_ref, table_ref, stage_ref, grads_ref, real)
        else:
            load_rows(rows, y_ref, table_ref, stage_ref, grads_ref, real, real)

    gate = dot_nn(rows_ref[...], gate_ref[...])
    up = dot_nn(rows_ref[...], up_ref[...])
    d_hidden = dot_nt(grads_ref[...], down_ref[...])
    sigmoid = jax.nn.sigmoid(gate)
    d_gate = (d_hidden * up * sigmoid * (1.0 + gate * (1.0 - sigmoid))).astype(jnp.bfloat16)
    d_up = (d_hidden * gate * sigmoid).astype(jnp.bfloat16)
    add_share(total_ref, dot_nt(d_gate, gate_ref[...]) + dot_nt(d_up, up_ref[...]))

    @pl.when(pl.program_id(0) == pl.num_programs(0) - 1)
    def _():
        store_rows(total_ref, y_ref, table_ref, stage_ref, out_ref)


def weight_specs(width, hidden):
    return [
        pl.BlockSpec((width, HIDDEN_BLOCK), lambda j, *_: (0, j)),
        pl.BlockSpec((width, HIDDEN_BLOCK), lambda j, *_: (0, j)),
        pl.BlockSpec((HIDDEN_BLOCK, width), lambda j, *_: (j, 0)),
    ]


def whole(shape):
    return pl.BlockSpec(shape, lambda j, *_: (0,) * len(shape))


def expert_call(kernel, column, rows, grads, grid, table, weights):
    width, hidden = weights[0].shape
    total = COLUMN * GROUP
    backward = kernel is backward_kernel
    inputs = list(rows) + list(grads) + [table]
    counts = (len(rows), len(grads)) if backward else (len(rows),)
    return pl.pallas_call(
        functools.partial(kernel, *counts),
        grid_spec=pltpu.PrefetchScalarGridSpec(
            num_scalar_prefetch=1,
            grid=(hidden // HIDDEN_BLOCK,),
            in_specs=[whole(v.shape) for v in inputs] + weight_specs(width, hidden),
            out_specs=whole(grid),
            scratch_shapes=[pltpu.VMEM((total, width), jnp.bfloat16)] * (2 if backward else 1)
            + [
                pltpu.VMEM((total, width), jnp.float32),
                pltpu.VMEM((PARTS * GROUP, grid[3]), jnp.bfloat16),
            ],
        ),
        out_shape=jax.ShapeDtypeStruct(grid, jnp.bfloat16),
        compiler_params=pltpu.CompilerParams(vmem_limit_bytes=VMEM_LIMIT),
        cost_estimate=pl.CostEstimate(
            flops=(10 if backward else 6) * total * width * hidden,
            bytes_accessed=6 * width * hidden,
            transcendentals=total * hidden,
        ),
        name="expert_backward" if backward else "expert_forward",
    )(column, *inputs, *weights)


def pick_kernel(z_ref, key_ref, *refs):
    blocks, outs, source_ref = refs[:-5], refs[-5:-1], refs[-1]
    lanes = key_ref.shape[1]
    for d, block in enumerate(blocks):
        tokens = block.shape[0]
        place = (z_ref[0] + d) % len(blocks) * tokens
        source_ref[pl.ds(pl.multiple_of(place, tokens), tokens), :] = block[...]
    slots = iota((GROUP, lanes), 0)
    hits = [key_ref[d : d + 1, :] == slots for d in range(len(outs))]
    rows = dot_nn(jnp.concatenate(hits, axis=0).astype(jnp.bfloat16), source_ref[...])
    for d, out in enumerate(outs):
        out[...] = rows[d * GROUP : d * GROUP + out.shape[0]].astype(jnp.bfloat16)


def pair_kernel(z_ref, key_ref, weight_ref, *refs):
    blocks, outs, source_ref = refs[:-5], refs[-5:-1], refs[-1]
    lanes = key_ref.shape[1]
    count = len(blocks) // 2
    slots = iota((GROUP, lanes), 0)
    hits = [key_ref[d : d + 1, :] == slots for d in range(len(outs))]
    real = outs[0].shape[0] // 2
    for stream in range(2):
        for d, block in enumerate(blocks[stream * count : (stream + 1) * count]):
            tokens = block.shape[0]
            place = (z_ref[0] + d) % count * tokens
            source_ref[pl.ds(pl.multiple_of(place, tokens), tokens), :] = block[...]
        if stream:
            table = [jnp.where(hit, weight_ref[d : d + 1, :], 0.0) for d, hit in enumerate(hits)]
            table = jnp.concatenate(table, axis=0)
            high = table.astype(jnp.bfloat16)
            low = (table - high.astype(jnp.float32)).astype(jnp.bfloat16)
            rows = dot_nn(high, source_ref[...]) + dot_nn(low, source_ref[...])
        else:
            rows = dot_nn(jnp.concatenate(hits, axis=0).astype(jnp.bfloat16), source_ref[...])
        for d, out in enumerate(outs):
            out[stream * real : (stream + 1) * real, :] = rows[d * GROUP : d * GROUP + real].astype(jnp.bfloat16)


def column_pick(kernel, at_z, tables, blocks, parts, tokens, real):
    width = blocks[0].shape[1]
    lanes = tables[0].shape[1]
    return pl.pallas_call(
        kernel,
        grid_spec=pltpu.PrefetchScalarGridSpec(
            num_scalar_prefetch=1,
            grid=(1,),
            in_specs=[whole(t.shape) for t in tables]
            + [pl.BlockSpec((tokens, width), lambda j, *_, part=part: (part, 0)) for part in parts],
            out_specs=[whole((real, width))] * 4,
            scratch_shapes=[pltpu.VMEM((lanes, width), jnp.bfloat16)],
        ),
        out_shape=[jax.ShapeDtypeStruct((real, width), jnp.bfloat16)] * 4,
        compiler_params=pltpu.CompilerParams(vmem_limit_bytes=VMEM_LIMIT),
        cost_estimate=pl.CostEstimate(
            flops=8 * GROUP * lanes * width, bytes_accessed=4 * lanes * width, transcendentals=0
        ),
        name="column_pick",
    )(at_z, *tables, *blocks)


def gathered_round(block, axis, cut, gates=None):
    gates = gates or {}
    half = lax.axis_size(axis) // 2
    up, down = block, block
    ahead, behind = [], []
    for r in range(1, half):
        if r in gates:
            up, down = after((up, down), gates[r])
        up, down = turned(up, axis, 1), turned(down, axis, -1)
        ahead.append(down)
        behind.append(up)
    if half in gates:
        up, down = after((up, down), gates[half])
    far = turned(up[:cut], axis, 1), turned(down[cut:], axis, -1)
    return [block] + ahead, far, behind[::-1]


def on_device(
    enter_fwd,
    held_fwd,
    route_fwd,
    prob_fwd,
    enter_grad,
    held_grad,
    saved_inputs,
    route_grad,
    prob_grad,
    norm_gain,
    w_gate,
    w_up,
    w_down,
):
    tokens = held_fwd.shape[1]
    width = held_fwd.shape[2]
    layers_z, layers_y = lax.axis_size("z"), lax.axis_size("y")
    at_z, at_y = lax.axis_index("z"), lax.axis_index("y")
    experts = layers_z * layers_y
    lanes = PARTS * tokens
    chunk = CAP * PARTS
    part = width // PARTS
    gain = norm_gain[0]
    gate_w, up_w, down_w = w_gate[0, 0], w_up[0, 0], w_down[0, 0]
    section = lax.axis_index("pipe")
    last_section = lax.axis_size("pipe") - 1

    def exchanged(chunks):
        return lax.all_to_all(chunks, ("z", "y"), split_axis=0, concat_axis=0, tiled=True)

    spread = (iota((tokens, lanes), 0) == iota((tokens, lanes), 1) % tokens).astype(jnp.bfloat16)
    choices = route_fwd.shape[-1]
    routes = jnp.concatenate([route_fwd[:, 0], route_grad[:, 0]]).transpose(0, 2, 1).astype(jnp.bfloat16)
    probs = jnp.concatenate([prob_fwd[:, 0], prob_grad[:, 0]]).transpose(0, 2, 1)
    earlier = earlier_tokens(lanes, tokens)
    column_owner = at_z * layers_y + (at_y + iota((layers_y, lanes), 0)) % layers_y

    wide_saved, scale_saved, normed_saved = norm_rows(
        saved_inputs[:, 0].reshape(STEPS * tokens, width), gain
    )
    wide, _, normed_fwd = norm_rows(held_fwd[0], gain)
    place = (iota((tokens, lanes), 0) + at_z * tokens == iota((tokens, lanes), 1)).astype(jnp.bfloat16)
    notes = [routes[0], routes[STEPS], routes[STEPS + 1]] + split_three(probs[STEPS])
    fields = len(notes)
    notes = jnp.dot(jnp.concatenate(notes), place, preferred_element_type=jnp.float32).astype(jnp.bfloat16)
    notes = jnp.concatenate(list(notes.reshape(fields, choices, lanes)), axis=1)
    notes = jnp.pad(notes, ((0, 0), (0, width - fields * lanes)))
    payload = jnp.concatenate([normed_saved[:tokens], held_grad[0], notes])
    ahead, far, behind = gathered_round(payload, "z", tokens)
    noted = far[1][tokens : tokens + choices].astype(jnp.float32)
    for block in ahead + behind:
        noted = noted + block[2 * tokens : 2 * tokens + choices].astype(jnp.float32)
    noted = [noted[:, i * lanes : (i + 1) * lanes] for i in range(fields)]

    def column_keys(route, prob):
        route = route.astype(jnp.int32)
        hit = jnp.zeros((layers_y, lanes), jnp.bool_)
        weight = None if prob is None else jnp.zeros((layers_y, lanes), jnp.float32)
        for k in range(choices):
            same = column_owner == route[k][None, :]
            hit = hit | same
            if prob is not None:
                weight = jnp.where(same, prob[k][None, :], weight)
        block = iota((layers_y, lanes), 1) // tokens
        return jnp.where(hit, ranked(hit, earlier) + block * CAP, -1), weight

    forward_keys = column_keys(noted[0], None)
    grad_keys = column_keys(noted[1], noted[3] + noted[4] + noted[5])
    later_keys = column_keys(noted[2], None)

    def column_sent(rows):
        return [rows[0]] + [turned(rows[d], "y", d) for d in range(1, layers_y)]

    row, column = at_z.astype(jnp.int32).reshape(1), at_y.astype(jnp.int32).reshape(1)

    real = layers_z * CAP
    blocks = [ahead + [far[i]] + behind for i in range(2)]
    parts = [[i] * len(ahead) + [0] + [i] * len(behind) for i in range(2)]
    rows_grad = column_pick(
        pair_kernel, row, grad_keys, blocks[0] + blocks[1], parts[0] + parts[1], tokens, 2 * real
    )
    come_pair = column_sent(rows_grad)
    fwd_ahead, fwd_far, fwd_behind = gathered_round(
        after(normed_fwd, rows_grad), "z", tokens // 2, {3: come_pair[1], 4: (come_pair[2], come_pair[3])}
    )

    saved_gathered = lax.all_gather(after(normed_saved[tokens:], far), "z", axis=0, tiled=True)

    route_lanes = jnp.dot(
        routes.reshape(-1, tokens), spread, preferred_element_type=jnp.float32
    )
    route_lanes = route_lanes.astype(jnp.int32).reshape(2 * STEPS, choices, lanes)
    prob_lanes = jnp.dot(
        probs.reshape(-1, tokens), spread.astype(jnp.float32), precision=lax.Precision.HIGHEST
    )
    prob_lanes = prob_lanes.reshape(2 * STEPS, choices, lanes)

    def forward_send(block, step):
        wide, _, normed = norm_rows(block, gain)
        key, _ = slot_keys(route_lanes[step], prob_lanes[step], experts, tokens, earlier)
        send = picked(select_table(key, chunk), to_parts(normed)).astype(jnp.bfloat16)
        return wide, send.reshape(experts, chunk, part)

    def forward_mixing(step):
        key, weight = slot_keys(route_lanes[step], prob_lanes[step], experts, tokens, earlier)
        return tuple(t.T for t in weight_table(key, weight, chunk))

    def grad_send(block, step):
        key, weight = slot_keys(
            route_lanes[STEPS + step], prob_lanes[STEPS + step], experts, tokens, earlier
        )
        high, low = weight_table(key, weight, chunk)
        parts = to_parts(block)
        send = (picked(high, parts) + picked(low, parts)).astype(jnp.bfloat16)
        return send.reshape(experts, chunk, part)

    def grad_select(step):
        key, _ = slot_keys(
            route_lanes[STEPS + step], prob_lanes[STEPS + step], experts, tokens, earlier
        )
        return select_table(key, chunk).T

    def forward_out(wide, mixing, back):
        high, low = mixing
        back = back.reshape(experts * chunk, part)
        return (wide + from_parts(picked(high, back) + picked(low, back), tokens)).astype(jnp.bfloat16)

    def grad_out(block, select, step, back):
        d_normed = from_parts(picked(select, back.reshape(experts * chunk, part)), tokens)
        mine = slice(step * tokens, (step + 1) * tokens)
        wide, scale = wide_saved[mine], scale_saved[mine]
        scaled_u = d_normed * gain[None, :]
        inner = jnp.mean(scaled_u * wide, axis=-1, keepdims=True)
        d_block = scale * scaled_u - wide * (scale * scale * scale) * inner
        return (block.astype(jnp.float32) + d_block).astype(jnp.bfloat16)

    table = regroup(PARTS, layers_z * CAP, GROUP)
    weights = (gate_w, up_w, down_w)
    grid = (layers_z, layers_y, chunk, part)
    flat = (experts, chunk, part)
    block_grad = held_grad[0]
    outputs_all, grads_all = [], []
    blocks = fwd_ahead + [jnp.concatenate(fwd_far)] + fwd_behind
    come_fwd = column_sent(
        column_pick(pick_kernel, row, [after(forward_keys[0], come_pair)], blocks, [0] * len(blocks), tokens, real)
    )
    result_grad = expert_call(backward_kernel, column, come_pair, [], grid, table, weights)
    mixing, select = forward_mixing(0), grad_select(0)
    ready = (come_fwd, saved_gathered)
    for step in range(STEPS):
        more = step + 1 < STEPS
        back_grad = exchanged(after(result_grad.reshape(flat), *ready))
        result_fwd = expert_call(forward_kernel, column, come_fwd, [], grid, table, weights)
        if more:
            rows_saved = column_pick(
                pick_kernel,
                jnp.zeros_like(row),
                [after(later_keys[0], come_fwd)],
                [saved_gathered],
                [0],
                lanes,
                real,
            )
            come_saved = column_sent(rows_saved)
        back_fwd = exchanged(after(result_fwd.reshape(flat), back_grad, come_saved))
        out_grad = grad_out(block_grad, select, step, back_grad)
        grads_all.append(out_grad[None])
        if more:
            moved_grad = passed_along(out_grad, "pipe", -1)
            block_grad = jnp.where(section == last_section, enter_grad[step], moved_grad)
            send_grad = grad_send(block_grad, step + 1)
            back_fwd, send_grad = lax.optimization_barrier((back_fwd, send_grad))
            come_grad = exchanged(send_grad)
        out_fwd = forward_out(wide, mixing, back_fwd)
        outputs_all.append(out_fwd[None])
        if more:
            moved_fwd = passed_along(out_fwd, "pipe", 1)
            block_fwd = jnp.where(section == 0, enter_fwd[step], moved_fwd)
            wide, send_fwd = forward_send(block_fwd, step + 1)
            mixing, select = forward_mixing(step + 1), grad_select(step + 1)
            come_fwd = [exchanged(after(send_fwd, come_grad)).reshape(grid)]
            result_grad = expert_call(
                backward_kernel, column, come_saved, [come_grad.reshape(grid)], grid, table, weights
            )
            ready = (come_fwd,)
    return (jnp.stack(outputs_all), jnp.stack(grads_all))


def solution(mesh):
    sections, owners = mesh.devices.shape
    grid = Mesh(mesh.devices.reshape(sections, owners // COLUMN, COLUMN), ("pipe", "z", "y"))
    expert = ("z", "y")
    return jax.shard_map(
        on_device,
        mesh=grid,
        in_specs=(
            P(None, expert, None),
            P("pipe", expert, None),
            P(None, "pipe", expert, None),
            P(None, "pipe", expert, None),
            P(None, expert, None),
            P("pipe", expert, None),
            P(None, "pipe", expert, None),
            P(None, "pipe", expert, None),
            P(None, "pipe", expert, None),
            P("pipe", None),
            P("pipe", expert, None, None),
            P("pipe", expert, None, None),
            P("pipe", expert, None, None),
        ),
        out_specs=(P(None, "pipe", expert, None), P(None, "pipe", expert, None)),
        check_vma=False,
    )
```
